512 devices in a mesh: ctx: 32 (over x, y, core), head: 16 (over z).
Axes of the slice: x: 4, y: 4, z: 16, core: 2. Of those that a mesh axis runs over, the one named last changes fastest.
Arguments:
- queries: bfloat16 [16384, 8192], P('ctx', 'head'), may hold values from -6 to 6
- key_rows: bfloat16 [16384, 8192], P('ctx', 'head'), may hold values from -6 to 6
- values: bfloat16 [16384, 8192], P('ctx', 'head'), may hold values from -7 to 7
- log_decay: float32 [64, 16384], P('head', 'ctx'), may hold values from -1.5 to 0, as said below
- norm_gain: float32 [8192], P('head'), may hold values from 0.25 to 1.75
- grad_normed: bfloat16 [16384, 8192], P('ctx', 'head'), may hold values from -6 to 6
Outputs:
- grad_queries: bfloat16 [16384, 8192], P('ctx', 'head')
- grad_keys: bfloat16 [16384, 8192], P('ctx', 'head')
- grad_values: bfloat16 [16384, 8192], P('ctx', 'head')
The draws below stay inside these ranges and needn't reach their ends.
Inputs may be any that keep to these rules, and one draw needn't show every extreme that they name: `log_decay`: every entry is the logarithm of a decay factor, so it is below zero.
All inputs are finite; a program needn't handle non-finite values.
Results may differ from the reference program's by a relative error of at most 0.0063.
Values sent between devices are 32-bit elements; how exact they have to be, the bound alone decides.
No kernel may reach another device: no remote copies, remote signals or barrier semaphores. Data moves between devices by JAX's collectives and lax.ppermute only.
A program may use at most 64 MiB of HBM per device.

```python
import math
import jax
import jax.numpy as jnp
from jax import lax

HEAD_COUNT = 64
HD = 128
TOK_DEV = 512
TOKEN_COUNT = 16384


def draw_log_decay(key, part):
    key = jax.random.fold_in(key, 7)
    every_key = jax.random.split(key, 7)
    head_kinds = jax.random.randint(every_key[0], (HEAD_COUNT,), 0, 20)
    slow_rate = jnp.exp(jax.random.uniform(every_key[1], (HEAD_COUNT,), minval=math.log(0.1), maxval=math.log(0.5))) / TOKEN_COUNT
    fast_rate = jnp.exp(jax.random.uniform(every_key[2], (HEAD_COUNT,), minval=math.log(1.0 / 50.0), maxval=math.log(1.0 / 30.0)))
    middle_rate = jnp.exp(jax.random.uniform(every_key[3], (HEAD_COUNT,), minval=math.log(4.0 / TOKEN_COUNT), maxval=math.log(1.0 / 50.0)))
    slow_heads = head_kinds < 10
    fast_heads = head_kinds >= 15
    block_factor = jnp.exp(jax.random.uniform(every_key[4], (HEAD_COUNT, TOKEN_COUNT // TOK_DEV), minval=math.log(0.5), maxval=math.log(2.0)))
    base_rate = jnp.where(slow_heads, slow_rate, jnp.where(fast_heads, fast_rate, middle_rate))
    decay_rates = jnp.repeat(base_rate[:, None] * block_factor, TOK_DEV, axis=1)
    spike_locations = jax.random.randint(every_key[5], (HEAD_COUNT, 2), 0, TOKEN_COUNT)
    spike_magnitude = jnp.log(jax.random.uniform(every_key[6], (HEAD_COUNT, 2), minval=0.5, maxval=0.8))
    token_positions = jnp.arange(TOKEN_COUNT)
    decay_spikes = jnp.sum(jnp.where(token_positions[None, None, :] == spike_locations[:, :, None], spike_magnitude[:, :, None], 0.0), axis=1)
    return (decay_spikes - decay_rates).astype(jnp.float32)


def draw_values(key, part):
    key = jax.random.fold_in(key, 23)
    columns = jnp.arange(HEAD_COUNT * HD) // HD
    base_draw = jnp.clip(jax.random.normal(key, (TOKEN_COUNT, HEAD_COUNT * HD)), -4.0, 4.0)
    rising = jnp.power(3.0, 0.5 * columns / max(HEAD_COUNT - 1, 1))
    return (base_draw * rising[None, :]).astype(jnp.float32).astype(jnp.bfloat16)


def levels(rng, shape, cuts, low, top_value):
    factor_of, own = 1.0, jax.random.fold_in(rng, 6)
    for position, blocks in cuts:
        heights = jnp.exp(jax.random.uniform(jax.random.fold_in(own, position), (blocks,), jnp.float32, low / len(cuts), top_value / len(cuts)))
        factor_of = factor_of * jnp.repeat(heights, shape[position] // blocks).reshape([-1 if axis == position else 1 for axis in range(len(shape))])
    return factor_of


def normal_values(key, extent, width, reach, pieces=(), kind=jnp.bfloat16):
    factor_of = levels(key, extent, pieces, -0.22, 0.18) if pieces else 1.0
    entries = jax.random.normal(key, extent, jnp.float32) * width * factor_of
    return jnp.minimum(jnp.maximum(entries, -reach), reach).astype(kind)


def setup_inputs(seed: int = 0) -> dict:
    streams_of = jax.random.split(jax.random.key(seed), 7)
    queries = normal_values(streams_of[0], (TOKEN_COUNT, HEAD_COUNT * HD), 1.0, 6.0, ((0, 32), (1, 16)))
    key_rows = normal_values(streams_of[1], (TOKEN_COUNT, HEAD_COUNT * HD), 1.0, 6.0, ((0, 32), (1, 16)))
    values = draw_values(jax.random.fold_in(streams_of[6], 71), 0)
    log_decay = draw_log_decay(jax.random.fold_in(streams_of[6], 71), 0)
    norm_gain = jnp.clip(1.0 + 0.15 * jax.random.normal(streams_of[4], (HEAD_COUNT * HD,), jnp.float32), 0.25, 1.75)
    grad_normed = normal_values(streams_of[5], (TOKEN_COUNT, HEAD_COUNT * HD), 1.0, 6.0, ((0, 32), (1, 16)))
    return {"queries": queries, "key_rows": key_rows, "values": values, "log_decay": log_decay, "norm_gain": norm_gain, "grad_normed": grad_normed}


EPSILON = 1e-05

def decay_table(log_rows):
    running = jnp.cumsum(log_rows, axis=1)
    length = log_rows.shape[1]
    token_positions = jnp.arange(length)
    causal = token_positions[:, None] >= token_positions[None, :]
    spread = running[:, :, None] - running[:, None, :]
    within = jnp.where(causal[None, :, :], jnp.exp(jnp.minimum(spread, 0.0)), 0.0)
    return (running, within)

def to_low(array_in):
    return lax.optimization_barrier(array_in.astype(jnp.bfloat16)).astype(jnp.float32)

def forward_block(state_now, inputs):
    query_block, key_block, value_block, log_rows = inputs
    running, within = decay_table(log_rows)
    block_total = running[:, -1]
    query_full = query_block.astype(jnp.float32)
    key_full = key_block.astype(jnp.float32)
    value_full = value_block.astype(jnp.float32)
    scores = jnp.einsum('thd,jhd->htj', query_full, key_full)
    masked = to_low(scores * within)
    state_low = to_low(state_now)
    local_part = jnp.einsum('htj,jhe->the', masked, value_full)
    carried = jnp.einsum('thd,hde->the', query_full, state_low)
    head_weight = jnp.exp(running).T[:, :, None]
    output = local_part + head_weight * carried
    tail_weight = jnp.exp(block_total[:, None] - running).T[:, :, None]
    scaled_keys = to_low(key_full * tail_weight)
    update = jnp.einsum('jhd,jhe->hde', scaled_keys, value_full)
    state_next = jnp.exp(block_total)[:, None, None] * state_now + update
    return (state_next, (output, state_now))

def backward_block(state_after, inputs):
    query_block, key_block, value_block, grad_block, log_rows, state_before = inputs
    running, within = decay_table(log_rows)
    block_total = running[:, -1]
    query_full = query_block.astype(jnp.float32)
    key_full = key_block.astype(jnp.float32)
    value_full = value_block.astype(jnp.float32)
    grad_full = grad_block.astype(jnp.float32)
    scores = jnp.einsum('thd,jhd->htj', query_full, key_full)
    masked = to_low(scores * within)
    pull_scores = jnp.einsum('the,jhe->htj', grad_full, value_full)
    pulled = to_low(pull_scores * within)
    head_weight = jnp.exp(running).T[:, :, None]
    tail_weight = jnp.exp(block_total[:, None] - running).T[:, :, None]
    state_low = to_low(state_before)
    out_low = to_low(state_after)
    grad_query = jnp.einsum('htj,jhd->thd', pulled, key_full) + head_weight * jnp.einsum('the,hde->thd', grad_full, state_low)
    grad_key = jnp.einsum('htj,thd->jhd', pulled, query_full) + tail_weight * jnp.einsum('jhe,hde->jhd', value_full, out_low)
    grad_value = jnp.einsum('htj,the->jhe', masked, grad_full) + tail_weight * jnp.einsum('jhd,hde->jhe', key_full, out_low)
    scaled_queries = to_low(query_full * head_weight)
    back_update = jnp.einsum('thd,the->hde', scaled_queries, grad_full)
    state_next = jnp.exp(block_total)[:, None, None] * state_after + back_update
    return (state_next, (grad_query.astype(jnp.bfloat16), grad_key.astype(jnp.bfloat16), grad_value.astype(jnp.bfloat16)))

def reference(queries, key_rows, values, log_decay, norm_gain, grad_normed):
    blocks = TOKEN_COUNT // TOK_DEV
    channels = HEAD_COUNT * HD

    def split_rows(array_in):
        return array_in.reshape(blocks, TOK_DEV, HEAD_COUNT, HD)
    logs = log_decay.reshape(HEAD_COUNT, blocks, TOK_DEV).transpose(1, 0, 2)
    zero_state = jnp.zeros((HEAD_COUNT, HD, HD), jnp.float32)
    final_state, (outputs, states_in) = lax.scan(forward_block, zero_state, (split_rows(queries), split_rows(key_rows), split_rows(values), logs))
    flat = outputs.reshape(TOKEN_COUNT, channels)
    mean_square = lax.optimization_barrier(jnp.sum(flat * flat, axis=1, keepdims=True)) / channels
    inverse = lax.rsqrt(mean_square + EPSILON)
    gained = grad_normed.astype(jnp.float32) * norm_gain.astype(jnp.float32)[None, :]
    inner_mean = lax.optimization_barrier(jnp.sum(flat * gained, axis=1, keepdims=True)) / channels
    grad_output = (inverse * gained - flat * (inverse * inverse * inverse * inner_mean)).astype(jnp.bfloat16)
    last_state, (grad_query, grad_key, grad_value) = lax.scan(backward_block, zero_state, (split_rows(queries), split_rows(key_rows), split_rows(values), split_rows(grad_output), logs, states_in), reverse=True)
    return (grad_query.reshape(TOKEN_COUNT, channels), grad_key.reshape(TOKEN_COUNT, channels), grad_value.reshape(TOKEN_COUNT, channels))
```

```python
import jax
import jax.numpy as jnp
from jax import lax
from jax.experimental import pallas as pl
from jax.experimental.pallas import tpu as pltpu
from jax.sharding import PartitionSpec as P

HD = 128
EPSILON = 1e-05
F32 = jnp.float32
BF16 = jnp.bfloat16
VMEM_BYTES = 56 * 1024 * 1024


def dot(lhs, rhs, lhs_dim, rhs_dim):
    return lax.dot_general(
        lhs, rhs, (((lhs_dim,), (rhs_dim,)), ((), ())), preferred_element_type=F32
    )


def call(body, out_shapes, *operands, flops=0):
    moved = sum(a.size * a.dtype.itemsize for a in operands)
    moved += sum(s.size * s.dtype.itemsize for s in out_shapes)
    whole = pl.BlockSpec(memory_space=pltpu.VMEM)
    return pl.pallas_call(
        body,
        out_shape=out_shapes,
        in_specs=[whole] * len(operands),
        out_specs=[whole] * len(out_shapes),
        compiler_params=pltpu.CompilerParams(vmem_limit_bytes=VMEM_BYTES),
        cost_estimate=pl.CostEstimate(flops=flops, bytes_accessed=moved, transcendentals=0),
    )(*operands)


def like(shape, dtype=F32):
    return jax.ShapeDtypeStruct(shape, dtype)


def head_columns(head):
    return slice(head * HD, (head + 1) * HD)


def update_kernel(log_ref, key_ref, value_ref, send_ref, row_ref, column_ref):
    heads, length = log_ref.shape
    logs = jnp.concatenate([log_ref[...], jnp.zeros((8 - heads, length), F32)], axis=0)
    pieces = length // HD
    stacked = jnp.concatenate([logs[:, head_columns(i)] for i in range(pieces)], axis=0)
    before = lax.broadcasted_iota(jnp.int32, (HD, HD), 0)
    after = lax.broadcasted_iota(jnp.int32, (HD, HD), 1)
    upper = jnp.where(before <= after, 1.0, 0.0).astype(F32)
    sums = jnp.dot(
        stacked, upper, precision=lax.Precision.HIGHEST, preferred_element_type=F32
    )
    parts = []
    offset = jnp.zeros((8, 1), F32)
    for i in range(pieces):
        part = sums[i * 8 : (i + 1) * 8] + offset
        offset = part[:, HD - 1 : HD]
        parts.append(part)
    running = jnp.concatenate(parts, axis=1)
    row_ref[...] = running
    stack = jnp.concatenate(
        [running, jnp.exp(running), jnp.exp(offset - running), jnp.zeros((HD - 24, length), F32)],
        axis=0,
    )
    columns = stack.T
    column_ref[...] = columns
    targets, rows = send_ref.shape[0], send_ref.shape[1] - 8
    per_head = targets // heads
    for head in range(heads):
        tail = columns[:, 16 + head : 17 + head]
        scaled = (key_ref[:, head_columns(head)].astype(F32) * tail).astype(BF16)
        update = dot(scaled, value_ref[:, head_columns(head)], 0, 0)
        here = slice(head * per_head, (head + 1) * per_head)
        send_ref[here, :rows] = update.reshape(per_head, rows, HD)
        send_ref[here, rows:] = jnp.broadcast_to(
            offset[head : head + 1][None], (per_head, 8, HD)
        )


def forward_kernel(got_ref, send_ref, total_ref):
    blocks, rows = send_ref.shape[:2]
    totals = got_ref[:, rows : rows + 1, :]
    total_ref[...] = jnp.broadcast_to(totals, total_ref.shape)
    factors = jnp.exp(totals)
    state = jnp.zeros((rows, HD), F32)
    for block in range(blocks):
        send_ref[block] = state
        state = factors[block] * state + got_ref[block, :rows]


def backward_kernel(got_ref, total_ref, send_ref):
    blocks, rows = send_ref.shape[:2]
    factors = jnp.exp(total_ref[:, :1, :])
    state = jnp.zeros((rows, HD), F32)
    for block in reversed(range(blocks)):
        send_ref[block] = state
        state = factors[block] * state + got_ref[block]


def within_block(column, row, diagonal):
    spread = column - row
    if not diagonal:
        return jnp.exp(jnp.minimum(spread, 0.0))
    size = spread.shape[0]
    later = lax.broadcasted_iota(jnp.int32, (size, size), 0)
    earlier = lax.broadcasted_iota(jnp.int32, (size, size), 1)
    return jnp.where(later >= earlier, jnp.exp(jnp.minimum(spread, 0.0)), 0.0)


TILE = 256


def tiles(length):
    return [
        (slice(t, t + TILE), slice(j, j + TILE), t == j)
        for t in range(0, length, TILE)
        for j in range(0, t + TILE, TILE)
    ]


def local_kernel(query_ref, key_ref, value_ref, row_ref, column_ref, local_ref):
    length = query_ref.shape[0]
    for head in range(query_ref.shape[1] // HD):
        cols = head_columns(head)
        sums = {}
        for t, j, diagonal in tiles(length):
            within = within_block(
                column_ref[t, head : head + 1], row_ref[head : head + 1, j], diagonal
            )
            scores = dot(query_ref[t, cols], key_ref[j, cols], 1, 1)
            masked = (scores * within).astype(BF16)
            part = dot(masked, value_ref[j, cols], 1, 0)
            sums[t.start] = sums[t.start] + part if t.start in sums else part
        for start, value in sums.items():
            local_ref[start : start + TILE, cols] = value


def output_kernel(
    query_ref, local_ref, state_ref, column_ref, normed_ref, gain_ref, output_ref, send_ref
):
    length = query_ref.shape[0]
    squares = jnp.zeros((length, HD), F32)
    crosses = jnp.zeros((length, HD), F32)
    for head in range(query_ref.shape[1] // HD):
        cols = head_columns(head)
        carried = dot(query_ref[:, cols], state_ref[cols].astype(BF16), 1, 0)
        output = local_ref[:, cols] + column_ref[:, 8 + head : 9 + head] * carried
        output_ref[:, cols] = output
        gained = normed_ref[:, cols].astype(F32) * gain_ref[:, cols]
        squares = squares + output * output
        crosses = crosses + output * gained
    sums = []
    for total in (squares, crosses):
        for i in range(length // HD):
            sums.append(jnp.sum(total[head_columns(i)].T, axis=0, keepdims=True))
    packed = jnp.concatenate(sums, axis=0)
    send_ref[...] = jnp.broadcast_to(packed[None], send_ref.shape)


def grad_kernel(
    sums_ref, output_ref, normed_ref, gain_ref, query_ref, column_ref, grad_ref, send_ref
):
    length = query_ref.shape[0]
    heads = query_ref.shape[1] // HD
    pieces = length // HD
    channels = sums_ref.shape[0] * heads * HD
    sums = jnp.sum(sums_ref[...], axis=0)
    inverse = lax.rsqrt(sums[:pieces] / channels + EPSILON)
    inner = sums[pieces:] / channels
    scale = inverse * inverse * inverse * inner
    both = jnp.concatenate([inverse, scale, jnp.zeros((HD - 2 * pieces, HD), F32)], axis=0).T
    inverse = jnp.concatenate([both[:, i : i + 1] for i in range(pieces)], axis=0)
    scale = jnp.concatenate([both[:, pieces + i : pieces + i + 1] for i in range(pieces)], axis=0)
    targets, rows = send_ref.shape[:2]
    per_head = targets // heads
    for head in range(heads):
        cols = head_columns(head)
        gained = normed_ref[:, cols].astype(F32) * gain_ref[:, cols]
        grad = (inverse * gained - output_ref[:, cols] * scale).astype(BF16)
        grad_ref[:, cols] = grad
        scaled = (query_ref[:, cols].astype(F32) * column_ref[:, 8 + head : 9 + head]).astype(BF16)
        send_ref[head * per_head : (head + 1) * per_head] = dot(scaled, grad, 0, 0).reshape(
            per_head, rows, HD
        )


def pull_kernel(
    query_ref,
    key_ref,
    value_ref,
    grad_ref,
    state_ref,
    row_ref,
    column_ref,
    grad_query_ref,
    key_part_ref,
    value_part_ref,
):
    length = query_ref.shape[0]

    def add(sums, where, part):
        sums[where] = sums[where] + part if where in sums else part

    for head in range(query_ref.shape[1] // HD):
        cols = head_columns(head)
        query_sums, key_sums, value_sums = {}, {}, {}
        for t, j, diagonal in tiles(length):
            within = within_block(
                column_ref[t, head : head + 1], row_ref[head : head + 1, j], diagonal
            )
            query, key, value, grad = (
                query_ref[t, cols],
                key_ref[j, cols],
                value_ref[j, cols],
                grad_ref[t, cols],
            )
            pulled = (dot(grad, value, 1, 1) * within).astype(BF16)
            masked = (dot(query, key, 1, 1) * within).astype(BF16)
            add(query_sums, t.start, dot(pulled, key, 1, 0))
            add(key_sums, j.start, dot(pulled, query, 0, 0))
            add(value_sums, j.start, dot(masked, grad, 0, 0))
        low = state_ref[cols].astype(BF16)
        for start in range(0, length, TILE):
            here = slice(start, start + TILE)
            carried = dot(grad_ref[here, cols], low, 1, 1)
            grad_query_ref[here, cols] = (
                query_sums[start] + column_ref[here, 8 + head : 9 + head] * carried
            ).astype(BF16)
            key_part_ref[here, cols] = key_sums[start]
            value_part_ref[here, cols] = value_sums[start]


def finish_kernel(
    key_part_ref, value_part_ref, key_ref, value_ref, state_ref, column_ref, grad_key_ref, grad_value_ref
):
    for head in range(key_ref.shape[1] // HD):
        cols = head_columns(head)
        low = state_ref[cols].astype(BF16)
        tail = column_ref[:, 16 + head : 17 + head]
        grad_key_ref[:, cols] = (
            key_part_ref[:, cols] + tail * dot(value_ref[:, cols], low, 1, 1)
        ).astype(BF16)
        grad_value_ref[:, cols] = (
            value_part_ref[:, cols] + tail * dot(key_ref[:, cols], low, 1, 0)
        ).astype(BF16)


def on_device(blocks, groups, queries, key_rows, values, log_decay, norm_gain, grad_normed):
    length, width = queries.shape
    heads = log_decay.shape[0]
    rows = heads * HD // blocks
    gain = norm_gain.reshape(1, width)
    square = 2 * length * length * HD * heads
    narrow = 2 * length * HD * HD * heads

    def swap(array, axis):
        return lax.all_to_all(array, axis, 0, 0, tiled=True)

    first, row, column = call(
        update_kernel,
        [like((blocks, rows + 8, HD)), like((8, length)), like((length, HD))],
        log_decay,
        key_rows,
        values,
        flops=narrow,
    )
    got = swap(first, "ctx")
    (local,) = call(
        local_kernel, [like((length, width))], queries, key_rows, values, row, column, flops=2 * square
    )
    states, totals = call(
        forward_kernel, [like((blocks, rows, HD)), like((blocks, 8, HD))], got
    )
    state_in = swap(states, "ctx").reshape(heads * HD, HD)
    output, sums = call(
        output_kernel,
        [like((length, width)), like((groups, 2 * length // HD, HD))],
        queries,
        local,
        state_in,
        column,
        grad_normed,
        gain,
        flops=narrow,
    )
    sums = swap(sums, "head")
    grad, second = call(
        grad_kernel,
        [like((length, width), BF16), like((blocks, rows, HD))],
        sums,
        output,
        grad_normed,
        gain,
        queries,
        column,
        flops=narrow,
    )
    got = swap(second, "ctx")
    grad_query, key_part, value_part = call(
        pull_kernel,
        [like((length, width), BF16), like((length, width)), like((length, width))],
        queries,
        key_rows,
        values,
        grad,
        state_in,
        row,
        column,
        flops=5 * square,
    )
    (states,) = call(backward_kernel, [like((blocks, rows, HD))], got, totals)
    state_out = swap(states, "ctx").reshape(heads * HD, HD)
    grad_key, grad_value = call(
        finish_kernel,
        [like((length, width), BF16), like((length, width), BF16)],
        key_part,
        value_part,
        key_rows,
        values,
        state_out,
        column,
        flops=2 * narrow,
    )
    return grad_query, grad_key, grad_value


def solution(mesh):
    blocks, groups = mesh.shape["ctx"], mesh.shape["head"]

    def run(*arrays):
        return on_device(blocks, groups, *arrays)

    return jax.shard_map(
        run,
        mesh=mesh,
        in_specs=(
            P("ctx", "head"),
            P("ctx", "head"),
            P("ctx", "head"),
            P("head", "ctx"),
            P("head"),
            P("ctx", "head"),
        ),
        out_specs=(P("ctx", "head"), P("ctx", "head"), P("ctx", "head")),
        check_vma=False,
    )
```

```python
import jax
import jax.numpy as jnp
from jax import lax
from jax.experimental import pallas as pl
from jax.experimental.pallas import tpu as pltpu
from jax.sharding import PartitionSpec as P

HD = 128
EPSILON = 1e-05
F32 = jnp.float32
BF16 = jnp.bfloat16
VMEM_BYTES = 16 * 1024 * 1024


def dot(lhs, rhs, lhs_dim, rhs_dim):
    return lax.dot_general(
        lhs, rhs, (((lhs_dim,), (rhs_dim,)), ((), ())), preferred_element_type=F32
    )


def call(body, out_shapes, *operands, flops=0, places_in={}, places_out={}, scratch=()):
    moved = sum(a.size * a.dtype.itemsize for a in operands)
    moved += sum(s.size * s.dtype.itemsize for s in out_shapes)

    def specs(count, outside):
        return [
            pl.BlockSpec(memory_space=outside.get(i, pltpu.VMEM)) for i in range(count)
        ]

    operands = [
        pltpu.with_memory_space_constraint(a, places_in[i]) if i in places_in else a
        for i, a in enumerate(operands)
    ]
    return pl.pallas_call(
        body,
        out_shape=[
            places_out[i](s.shape, s.dtype) if i in places_out else s
            for i, s in enumerate(out_shapes)
        ],
        in_specs=specs(len(operands), places_in),
        out_specs=specs(len(out_shapes), places_out),
        scratch_shapes=scratch,
        compiler_params=pltpu.CompilerParams(vmem_limit_bytes=VMEM_BYTES),
        cost_estimate=pl.CostEstimate(flops=flops, bytes_accessed=moved, transcendentals=0),
    )(*operands)


def like(shape, dtype=F32):
    return jax.ShapeDtypeStruct(shape, dtype)


def head_columns(head):
    return slice(head * HD, (head + 1) * HD)


def turn(rows):
    return jnp.concatenate([rows, jnp.zeros((HD - 8, rows.shape[1]), F32)], axis=0).T


def tail_rows(row_ref):
    running = row_ref[...]
    return jnp.exp(running[:, running.shape[1] - 1 :] - running)


def load_columns(sources, buffers, semaphores):
    copies = []
    for which, (source, buffer) in enumerate(zip(sources, buffers)):
        copies.append([])
        for head in range(source.shape[1] // HD):
            cols = head_columns(head)
            copy = pltpu.make_async_copy(
                source.at[:, cols], buffer.at[:, cols], semaphores.at[which, head]
            )
            copies[which].append(copy)
    for head in zip(*copies):
        for copy in head:
            copy.start()
    return copies


def update_kernel(
    log_in,
    key_in,
    value_in,
    send_ref,
    row_ref,
    log_ref,
    log_semaphore,
    key_ref,
    value_ref,
    semaphores,
):
    load_logs = pltpu.make_async_copy(log_in, log_ref, log_semaphore)
    load_logs.start()
    loads = load_columns((key_in, value_in), (key_ref, value_ref), semaphores)
    heads, length = log_ref.shape
    load_logs.wait()
    logs = jnp.concatenate([log_ref[...], jnp.zeros((8 - heads, length), F32)], axis=0)
    pieces = length // HD
    stacked = jnp.concatenate([logs[:, head_columns(i)] for i in range(pieces)], axis=0)
    high = stacked.astype(BF16)
    rest = stacked - high.astype(F32)
    middle = rest.astype(BF16)
    low = (rest - middle.astype(F32)).astype(BF16)
    before = lax.broadcasted_iota(jnp.int32, (HD, HD), 0)
    after = lax.broadcasted_iota(jnp.int32, (HD, HD), 1)
    upper = jnp.where(before <= after, 1.0, 0.0).astype(BF16)
    three = dot(jnp.concatenate([high, middle, low], axis=0), upper, 1, 0)
    count = 8 * pieces
    sums = (three[2 * count :] + three[count : 2 * count]) + three[:count]
    parts = []
    offset = jnp.zeros((8, 1), F32)
    for i in range(pieces):
        part = sums[i * 8 : (i + 1) * 8] + offset
        offset = part[:, HD - 1 : HD]
        parts.append(part)
    running = jnp.concatenate(parts, axis=1)
    row_ref[...] = running
    tail = jnp.exp(offset - running)
    targets, rows = send_ref.shape[0], send_ref.shape[1] - 8
    per_head = targets // heads
    for head in range(heads):
        here = slice(head * per_head, (head + 1) * per_head)
        send_ref[here, rows:] = jnp.broadcast_to(
            offset[head : head + 1][None], (per_head, 8, HD)
        )
    for head in range(heads):
        for load in loads:
            load[head].wait()
        turned = key_ref[:, head_columns(head)].T.astype(F32)
        scaled = (turned * tail[head : head + 1]).astype(BF16)
        update = dot(scaled, value_ref[:, head_columns(head)], 1, 0)
        here = slice(head * per_head, (head + 1) * per_head)
        send_ref[here, :rows] = update.reshape(per_head, rows, HD)


def forward_kernel(got_ref, send_ref, total_ref):
    blocks, rows = send_ref.shape[:2]
    totals = got_ref[:, rows : rows + 1, :]
    total_ref[...] = jnp.broadcast_to(totals, total_ref.shape)
    factors = jnp.exp(totals)
    state = jnp.zeros((rows, HD), F32)
    for block in range(blocks):
        send_ref[block] = state
        state = factors[block] * state + got_ref[block, :rows]


def backward_kernel(got_ref, total_ref, send_ref):
    blocks, rows = send_ref.shape[:2]
    factors = jnp.exp(total_ref[:, :1, :])
    state = jnp.zeros((rows, HD), F32)
    for block in reversed(range(blocks)):
        send_ref[block] = state
        state = factors[block] * state + got_ref[block]


def within_block(column, row, diagonal):
    spread = column - row
    if not diagonal:
        return jnp.exp(jnp.minimum(spread, 0.0))
    size = spread.shape[0]
    later = lax.broadcasted_iota(jnp.int32, (size, size), 0)
    earlier = lax.broadcasted_iota(jnp.int32, (size, size), 1)
    return jnp.where(later >= earlier, jnp.exp(jnp.minimum(spread, 0.0)), 0.0)


TILE = 256


def tiles(length):
    return [
        (slice(t, t + TILE), slice(j, j + TILE), t == j)
        for t in range(0, length, TILE)
        for j in range(0, t + TILE, TILE)
    ]


def local_kernel(
    query_in,
    key_in,
    value_in,
    row_ref,
    gain_in,
    local_ref,
    column_ref,
    gain_ref,
    query_ref,
    key_ref,
    value_ref,
    semaphores,
):
    length = query_ref.shape[0]
    loads = load_columns(
        (query_in, key_in, value_in), (query_ref, key_ref, value_ref), semaphores
    )
    gain_ref[...] = jnp.broadcast_to(gain_in[...], gain_ref.shape)
    running = row_ref[...]
    column_ref[...] = jnp.concatenate(
        [running, jnp.exp(running), jnp.zeros((HD - 16, length), F32)], axis=0
    ).T
    for head in range(query_ref.shape[1] // HD):
        for load in loads:
            load[head].wait()
        cols = head_columns(head)
        sums = {}
        for t, j, diagonal in tiles(length):
            within = within_block(
                column_ref[t, head : head + 1], row_ref[head : head + 1, j], diagonal
            )
            scores = dot(query_ref[t, cols], key_ref[j, cols], 1, 1)
            masked = (scores * within).astype(BF16)
            part = dot(masked, value_ref[j, cols], 1, 0)
            sums[t.start] = sums[t.start] + part if t.start in sums else part
        for start, value in sums.items():
            local_ref[start : start + TILE, cols] = value


def output_kernel(
    query_ref, local_ref, state_ref, column_ref, normed_ref, gain_ref, output_ref, send_ref, low_ref
):
    length = query_ref.shape[0]
    low_ref[...] = state_ref[...].reshape(low_ref.shape).astype(BF16)
    squares = jnp.zeros((length, HD), F32)
    crosses = jnp.zeros((length, HD), F32)
    for head in range(query_ref.shape[1] // HD):
        cols = head_columns(head)
        carried = dot(query_ref[:, cols], low_ref[cols], 1, 0)
        output = local_ref[:, cols] + column_ref[:, 8 + head : 9 + head] * carried
        output_ref[:, cols] = output
        gained = normed_ref[:, cols].astype(F32) * gain_ref[:1, cols]
        squares = squares + output * output
        crosses = crosses + output * gained
    sums = []
    for total in (squares, crosses):
        for i in range(length // HD):
            sums.append(jnp.sum(total[head_columns(i)].T, axis=0, keepdims=True))
    packed = jnp.concatenate(sums, axis=0)
    send_ref[...] = jnp.broadcast_to(packed[None], send_ref.shape)


def grad_kernel(
    sums_ref, output_ref, normed_ref, gain_ref, query_ref, column_ref, grad_ref, send_ref
):
    length = query_ref.shape[0]
    heads = query_ref.shape[1] // HD
    pieces = length // HD
    channels = sums_ref.shape[0] * heads * HD
    sums = jnp.sum(sums_ref[...], axis=0)
    inverse = lax.rsqrt(sums[:pieces] / channels + EPSILON)
    inner = sums[pieces:] / channels
    scale = inverse * inverse * inverse * inner
    both = jnp.concatenate([inverse, scale, jnp.zeros((HD - 2 * pieces, HD), F32)], axis=0).T
    inverse = jnp.concatenate([both[:, i : i + 1] for i in range(pieces)], axis=0)
    scale = jnp.concatenate([both[:, pieces + i : pieces + i + 1] for i in range(pieces)], axis=0)
    targets, rows = send_ref.shape[:2]
    per_head = targets // heads
    for head in range(heads):
        cols = head_columns(head)
        gained = normed_ref[:, cols].astype(F32) * gain_ref[:1, cols]
        grad = (inverse * gained - output_ref[:, cols] * scale).astype(BF16)
        grad_ref[:, cols] = grad
        scaled = (query_ref[:, cols].astype(F32) * column_ref[:, 8 + head : 9 + head]).astype(BF16)
        send_ref[head * per_head : (head + 1) * per_head] = dot(scaled, grad, 0, 0).reshape(
            per_head, rows, HD
        )


def add(sums, where, part):
    sums[where] = sums[where] + part if where in sums else part


def pull_kernel(
    query_in,
    key_in,
    value_in,
    grad_ref,
    low_ref,
    row_ref,
    grad_query_out,
    key_part_ref,
    value_part_ref,
    query_ref,
    key_ref,
    value_ref,
    semaphores,
    grad_query_ref,
    store_semaphores,
):
    length = query_ref.shape[0]
    loads = load_columns(
        (query_in, key_in, value_in), (query_ref, key_ref, value_ref), semaphores
    )
    stores = []
    columns, grown = turn(row_ref[...]), turn(jnp.exp(row_ref[...]))
    for head in range(query_ref.shape[1] // HD):
        for load in loads:
            load[head].wait()
        cols = head_columns(head)
        query_sums, key_sums, value_sums = {}, {}, {}
        for t, j, diagonal in tiles(length):
            within = within_block(
                columns[t, head : head + 1], row_ref[head : head + 1, j], diagonal
            )
            query, key, grad = query_ref[t, cols], key_ref[j, cols], grad_ref[t, cols]
            pulled = (dot(grad, value_ref[j, cols], 1, 1) * within).astype(BF16)
            masked = (dot(query, key, 1, 1) * within).astype(BF16)
            add(query_sums, t.start, dot(pulled, key, 1, 0))
            add(key_sums, j.start, dot(pulled, query, 0, 0))
            add(value_sums, j.start, dot(masked, grad, 0, 0))
        for start in range(0, length, TILE):
            here = slice(start, start + TILE)
            carried = dot(grad_ref[here, cols], low_ref[cols], 1, 1)
            grad_query_ref[here, cols] = (
                query_sums[start] + grown[here, head : head + 1] * carried
            ).astype(BF16)
            key_part_ref[here, cols] = key_sums[start]
            value_part_ref[here, cols] = value_sums[start]
        stores.append(
            pltpu.make_async_copy(
                grad_query_ref.at[:, cols], grad_query_out.at[:, cols], store_semaphores.at[head]
            )
        )
        stores[-1].start()
    for store in stores:
        store.wait()


def finish_kernel(
    key_part_ref,
    value_part_ref,
    key_ref,
    value_ref,
    state_ref,
    row_ref,
    grad_key_out,
    grad_value_out,
    grad_key_ref,
    grad_value_ref,
    semaphores,
):
    low = state_ref[...].reshape(-1, HD).astype(BF16)
    stores = []
    tails = turn(tail_rows(row_ref))
    for head in range(key_ref.shape[1] // HD):
        cols = head_columns(head)
        tail = tails[:, head : head + 1]
        grad_key_ref[:, cols] = (
            key_part_ref[:, cols] + tail * dot(value_ref[:, cols], low[cols], 1, 1)
        ).astype(BF16)
        grad_value_ref[:, cols] = (
            value_part_ref[:, cols] + tail * dot(key_ref[:, cols], low[cols], 1, 0)
        ).astype(BF16)
        for which, (source, target) in enumerate(
            ((grad_key_ref, grad_key_out), (grad_value_ref, grad_value_out))
        ):
            store = pltpu.make_async_copy(
                source.at[:, cols], target.at[:, cols], semaphores.at[2 * head + which]
            )
            store.start()
            stores.append(store)
    for store in stores:
        store.wait()


def on_device(blocks, groups, queries, key_rows, values, log_decay, norm_gain, grad_normed):
    length, width = queries.shape
    heads = log_decay.shape[0]
    rows = heads * HD // blocks
    gain = norm_gain.reshape(1, width)
    square = 2 * length * length * HD * heads
    narrow = 2 * length * HD * HD * heads

    def swap(array, axis):
        return lax.all_to_all(array, axis, 0, 0, tiled=True)

    whole = (length, width)
    block = pltpu.VMEM(whole, BF16)
    three = [block, block, block, pltpu.SemaphoreType.DMA((3, heads))]
    first, row = call(
        update_kernel,
        [like((blocks, rows + 8, HD)), like((8, length))],
        log_decay,
        key_rows,
        values,
        flops=narrow,
        places_in={0: pltpu.HBM, 1: pltpu.HBM, 2: pltpu.HBM},
        scratch=[
            pltpu.VMEM(log_decay.shape, F32),
            pltpu.SemaphoreType.DMA,
            block,
            block,
            pltpu.SemaphoreType.DMA((2, heads)),
        ],
    )
    got = swap(first, "ctx")
    local, column, gain = call(
        local_kernel,
        [like(whole), like((length, HD)), like((8, width))],
        queries,
        key_rows,
        values,
        row,
        gain,
        flops=2 * square,
        places_in={0: pltpu.HBM, 1: pltpu.HBM, 2: pltpu.HBM},
        scratch=three,
    )
    states, totals = call(
        forward_kernel,
        [like((blocks, rows, HD)), like((blocks, 8, HD))],
        got,
    )
    state_in = swap(states, "ctx")
    output, sums, low = call(
        output_kernel,
        [like(whole), like((groups, 2 * length // HD, HD)), like((heads * HD, HD), BF16)],
        queries,
        local,
        state_in,
        column,
        grad_normed,
        gain,
        flops=narrow,
    )
    sums = swap(sums, "head")
    grad, second = call(
        grad_kernel,
        [like(whole, BF16), like((blocks, rows, HD))],
        sums,
        output,
        grad_normed,
        gain,
        queries,
        column,
        flops=narrow,
    )
    got = swap(second, "ctx")
    (states,) = call(
        backward_kernel,
        [like((blocks, rows, HD))],
        got,
        totals,
    )
    state_out = swap(states, "ctx")
    grad_query, key_part, value_part = call(
        pull_kernel,
        [like(whole, BF16), like(whole), like(whole)],
        queries,
        key_rows,
        values,
        grad,
        low,
        row,
        flops=5 * square,
        places_in={0: pltpu.HBM, 1: pltpu.HBM, 2: pltpu.HBM},
        places_out={0: pltpu.HBM},
        scratch=[*three, block, pltpu.SemaphoreType.DMA((heads,))],
    )
    grad_key, grad_value = call(
        finish_kernel,
        [like(whole, BF16), like(whole, BF16)],
        key_part,
        value_part,
        key_rows,
        values,
        state_out,
        row,
        flops=2 * narrow,
        places_out={0: pltpu.HBM, 1: pltpu.HBM},
        scratch=[block, block, pltpu.SemaphoreType.DMA((2 * heads,))],
    )
    return grad_query, grad_key, grad_value


def solution(mesh):
    blocks, groups = mesh.shape["ctx"], mesh.shape["head"]

    def run(*arrays):
        return on_device(blocks, groups, *arrays)

    return jax.shard_map(
        run,
        mesh=mesh,
        in_specs=(
            P("ctx", "head"),
            P("ctx", "head"),
            P("ctx", "head"),
            P("head", "ctx"),
            P("head"),
            P("ctx", "head"),
        ),
        out_specs=(P("ctx", "head"), P("ctx", "head"), P("ctx", "head")),
        check_vma=False,
    )
```

```python
import functools

import jax
import jax.numpy as jnp
from jax import lax
from jax.experimental import pallas as pl
from jax.experimental.pallas import tpu as pltpu
from jax.sharding import PartitionSpec as P

HD = 128
EPSILON = 1e-05
F32 = jnp.float32
BF16 = jnp.bfloat16
VMEM_BYTES = 16 * 1024 * 1024


def dot(lhs, rhs, lhs_dim, rhs_dim):
    return lax.dot_general(
        lhs, rhs, (((lhs_dim,), (rhs_dim,)), ((), ())), preferred_element_type=F32
    )


def call(body, out_shapes, *operands, flops=0, places_in={}, places_out={}, scratch=()):
    moved = sum(a.size * a.dtype.itemsize for a in operands)
    moved += sum(s.size * s.dtype.itemsize for s in out_shapes)

    def specs(count, outside):
        return [
            pl.BlockSpec(memory_space=outside.get(i, pltpu.VMEM)) for i in range(count)
        ]

    operands = [
        pltpu.with_memory_space_constraint(a, places_in[i]) if i in places_in else a
        for i, a in enumerate(operands)
    ]
    return pl.pallas_call(
        body,
        out_shape=[
            places_out[i](s.shape, s.dtype) if i in places_out else s
            for i, s in enumerate(out_shapes)
        ],
        in_specs=specs(len(operands), places_in),
        out_specs=specs(len(out_shapes), places_out),
        scratch_shapes=scratch,
        compiler_params=pltpu.CompilerParams(vmem_limit_bytes=VMEM_BYTES),
        cost_estimate=pl.CostEstimate(flops=flops, bytes_accessed=moved, transcendentals=0),
    )(*operands)


def like(shape, dtype=F32):
    return jax.ShapeDtypeStruct(shape, dtype)


def head_columns(head):
    return slice(head * HD, (head + 1) * HD)


def turn(rows):
    return jnp.concatenate([rows, jnp.zeros((HD - 8, rows.shape[1]), F32)], axis=0).T


def tail_rows(row_ref):
    running = row_ref[...]
    return jnp.exp(running[:, running.shape[1] - 1 :] - running)


def load_all(sources, buffers, semaphores):
    loads = [
        pltpu.make_async_copy(source, buffer, semaphores.at[i])
        for i, (source, buffer) in enumerate(zip(sources, buffers))
    ]
    for load in loads:
        load.start()
    return loads


def update_kernel(
    targets,
    log_in,
    key_in,
    value_in,
    send_ref,
    row_ref,
    log_ref,
    log_semaphore,
    key_ref,
    value_ref,
    semaphores,
):
    load_logs = pltpu.make_async_copy(log_in, log_ref, log_semaphore)
    load_logs.start()
    loads = load_all((key_in, value_in), (key_ref, value_ref), semaphores)
    heads, length = log_ref.shape
    load_logs.wait()
    logs = jnp.concatenate([log_ref[...], jnp.zeros((8 - heads, length), F32)], axis=0)
    pieces = length // HD
    stacked = jnp.concatenate([logs[:, head_columns(i)] for i in range(pieces)], axis=0)
    high = stacked.astype(BF16)
    rest = stacked - high.astype(F32)
    middle = rest.astype(BF16)
    low = (rest - middle.astype(F32)).astype(BF16)
    before = lax.broadcasted_iota(jnp.int32, (HD, HD), 0)
    after = lax.broadcasted_iota(jnp.int32, (HD, HD), 1)
    upper = jnp.where(before <= after, 1.0, 0.0).astype(BF16)
    three = dot(jnp.concatenate([high, middle, low], axis=0), upper, 1, 0)
    count = 8 * pieces
    sums = (three[2 * count :] + three[count : 2 * count]) + three[:count]
    parts = []
    offset = jnp.zeros((8, 1), F32)
    for i in range(pieces):
        part = sums[i * 8 : (i + 1) * 8] + offset
        offset = part[:, HD - 1 : HD]
        parts.append(part)
    running = jnp.concatenate(parts, axis=1)
    row_ref[...] = running
    tail = jnp.exp(offset - running)
    per_head = targets // heads
    rows = heads * HD // targets
    for target in range(targets):
        last = target * (rows + 1) + rows
        head = target // per_head
        send_ref[last : last + 1] = jnp.broadcast_to(offset[head : head + 1], (1, HD))
    for load in loads:
        load.wait()
    for head in range(heads):
        turned = key_ref[:, head_columns(head)].T.astype(F32)
        scaled = (turned * tail[head : head + 1]).astype(BF16)
        update = dot(scaled, value_ref[:, head_columns(head)], 1, 0)
        for i in range(per_head):
            first = (head * per_head + i) * (rows + 1)
            send_ref[first : first + rows] = update[i * rows : (i + 1) * rows]


def forward_kernel(got_ref, send_ref, total_ref):
    blocks, rows = send_ref.shape[:2]
    state = jnp.zeros((rows, HD), F32)
    for block in range(blocks):
        first = block * (rows + 1)
        send_ref[block] = state
        total = got_ref[first + rows : first + rows + 1]
        total_ref[block] = jnp.broadcast_to(total, total_ref.shape[1:])
        state = jnp.exp(total) * state + got_ref[first : first + rows]


def backward_kernel(got_ref, total_ref, send_ref):
    blocks, rows = send_ref.shape[:2]
    factors = jnp.exp(total_ref[:, :1, :])
    state = jnp.zeros((rows, HD), F32)
    for block in reversed(range(blocks)):
        send_ref[block] = state
        state = factors[block] * state + got_ref[block]


def within_block(column, row, diagonal):
    spread = column - row
    if not diagonal:
        return jnp.exp(jnp.minimum(spread, 0.0))
    size = spread.shape[0]
    later = lax.broadcasted_iota(jnp.int32, (size, size), 0)
    earlier = lax.broadcasted_iota(jnp.int32, (size, size), 1)
    return jnp.where(later >= earlier, jnp.exp(jnp.minimum(spread, 0.0)), 0.0)


TILE = 256


def tiles(length):
    return [
        (slice(t, t + TILE), slice(j, j + TILE), t == j)
        for t in range(0, length, TILE)
        for j in range(0, t + TILE, TILE)
    ]


def local_kernel(
    query_in,
    key_in,
    value_in,
    row_ref,
    gain_in,
    local_ref,
    column_ref,
    gain_ref,
    turned_out,
    query_ref,
    key_ref,
    value_ref,
    semaphores,
    turned_ref,
    store_semaphore,
):
    length = query_ref.shape[0]
    loads = load_all((query_in, key_in, value_in), (query_ref, key_ref, value_ref), semaphores)
    gain_ref[...] = jnp.broadcast_to(gain_in[...], gain_ref.shape)
    running = row_ref[...]
    column_ref[...] = jnp.concatenate(
        [running, jnp.exp(running), jnp.zeros((HD - 16, length), F32)], axis=0
    ).T
    for load in loads:
        load.wait()
    for head in range(query_ref.shape[1] // HD):
        cols = head_columns(head)
        grown = jnp.exp(running[head : head + 1])
        turned_ref[cols] = (query_ref[:, cols].T.astype(F32) * grown).astype(BF16)
    store = pltpu.make_async_copy(turned_ref, turned_out, store_semaphore)
    store.start()
    for head in range(query_ref.shape[1] // HD):
        cols = head_columns(head)
        sums = {}
        for t, j, diagonal in tiles(length):
            within = within_block(
                column_ref[t, head : head + 1], row_ref[head : head + 1, j], diagonal
            )
            scores = dot(query_ref[t, cols], key_ref[j, cols], 1, 1)
            masked = (scores * within).astype(BF16)
            part = dot(masked, value_ref[j, cols], 1, 0)
            sums[t.start] = sums[t.start] + part if t.start in sums else part
        for start, value in sums.items():
            local_ref[start : start + TILE, cols] = value
    store.wait()


def output_kernel(
    query_ref, local_ref, state_ref, column_ref, normed_ref, gain_ref, output_ref, send_ref, low_ref
):
    length = query_ref.shape[0]
    low_ref[...] = state_ref[...].reshape(low_ref.shape).astype(BF16)
    squares = jnp.zeros((length, HD), F32)
    crosses = jnp.zeros((length, HD), F32)
    for head in range(query_ref.shape[1] // HD):
        cols = head_columns(head)
        carried = dot(query_ref[:, cols], low_ref[cols], 1, 0)
        output = local_ref[:, cols] + column_ref[:, 8 + head : 9 + head] * carried
        output_ref[:, cols] = output
        gained = normed_ref[:, cols].astype(F32) * gain_ref[:1, cols]
        squares = squares + output * output
        crosses = crosses + output * gained
    sums = []
    for total in (squares, crosses):
        for i in range(length // HD):
            sums.append(jnp.sum(total[head_columns(i)].T, axis=0, keepdims=True))
    packed = jnp.concatenate(sums, axis=0)
    send_ref[...] = jnp.broadcast_to(packed[None], send_ref.shape)


def grad_kernel(sums_ref, output_ref, normed_ref, gain_ref, turned_ref, grad_ref, send_ref):
    length, width = output_ref.shape
    heads = width // HD
    pieces = length // HD
    channels = sums_ref.shape[0] * width
    sums = jnp.sum(sums_ref[...], axis=0)
    inverse = lax.rsqrt(sums[:pieces] / channels + EPSILON)
    inner = sums[pieces:] / channels
    scale = inverse * inverse * inverse * inner

    def down(rows):
        return jnp.concatenate(
            [jnp.broadcast_to(rows[i : i + 1], (HD, HD)).T for i in range(pieces)], axis=0
        )

    inverse, scale = down(inverse), down(scale)
    targets, rows = send_ref.shape[:2]
    per_head = targets // heads
    for head in range(heads):
        cols = head_columns(head)
        gained = normed_ref[:, cols].astype(F32) * gain_ref[:1, cols]
        grad = (inverse * gained - output_ref[:, cols] * scale).astype(BF16)
        grad_ref[:, cols] = grad
        send_ref[head * per_head : (head + 1) * per_head] = dot(
            turned_ref[cols], grad, 1, 0
        ).reshape(per_head, rows, HD)


def add(sums, where, part):
    sums[where] = sums[where] + part if where in sums else part


def pull_kernel(
    query_in,
    key_in,
    value_in,
    grad_ref,
    low_ref,
    row_ref,
    grad_query_out,
    key_part_ref,
    value_part_ref,
    query_ref,
    key_ref,
    value_ref,
    semaphores,
    grad_query_ref,
    store_semaphores,
):
    length = query_ref.shape[0]
    loads = load_all((query_in, key_in, value_in), (query_ref, key_ref, value_ref), semaphores)
    stores = []
    columns, grown = turn(row_ref[...]), turn(jnp.exp(row_ref[...]))
    for load in loads:
        load.wait()
    for head in range(query_ref.shape[1] // HD):
        cols = head_columns(head)
        query_sums, key_sums, value_sums = {}, {}, {}
        for t, j, diagonal in tiles(length):
            within = within_block(
                columns[t, head : head + 1], row_ref[head : head + 1, j], diagonal
            )
            query, key, grad = query_ref[t, cols], key_ref[j, cols], grad_ref[t, cols]
            pulled = (dot(grad, value_ref[j, cols], 1, 1) * within).astype(BF16)
            masked = (dot(query, key, 1, 1) * within).astype(BF16)
            add(query_sums, t.start, dot(pulled, key, 1, 0))
            add(key_sums, j.start, dot(pulled, query, 0, 0))
            add(value_sums, j.start, dot(masked, grad, 0, 0))
        for start in range(0, length, TILE):
            here = slice(start, start + TILE)
            carried = dot(grad_ref[here, cols], low_ref[cols], 1, 1)
            grad_query_ref[here, cols] = (
                query_sums[start] + grown[here, head : head + 1] * carried
            ).astype(BF16)
            key_part_ref[here, cols] = key_sums[start]
            value_part_ref[here, cols] = value_sums[start]
        stores.append(
            pltpu.make_async_copy(
                grad_query_ref.at[:, cols], grad_query_out.at[:, cols], store_semaphores.at[head]
            )
        )
        stores[-1].start()
    for store in stores:
        store.wait()


def finish_kernel(
    key_part_ref,
    value_part_ref,
    key_ref,
    value_ref,
    state_ref,
    row_ref,
    grad_key_out,
    grad_value_out,
    grad_key_ref,
    grad_value_ref,
    semaphores,
):
    low = state_ref[...].reshape(-1, HD).astype(BF16)
    stores = []
    tails = turn(tail_rows(row_ref))
    for head in range(key_ref.shape[1] // HD):
        cols = head_columns(head)
        tail = tails[:, head : head + 1]
        grad_key_ref[:, cols] = (
            key_part_ref[:, cols] + tail * dot(value_ref[:, cols], low[cols], 1, 1)
        ).astype(BF16)
        grad_value_ref[:, cols] = (
            value_part_ref[:, cols] + tail * dot(key_ref[:, cols], low[cols], 1, 0)
        ).astype(BF16)
        for which, (source, target) in enumerate(
            ((grad_key_ref, grad_key_out), (grad_value_ref, grad_value_out))
        ):
            store = pltpu.make_async_copy(
                source.at[:, cols], target.at[:, cols], semaphores.at[2 * head + which]
            )
            store.start()
            stores.append(store)
    for store in stores:
        store.wait()


def on_device(blocks, groups, queries, key_rows, values, log_decay, norm_gain, grad_normed):
    length, width = queries.shape
    heads = log_decay.shape[0]
    rows = heads * HD // blocks
    gain = norm_gain.reshape(1, width)
    square = 2 * length * length * HD * heads
    narrow = 2 * length * HD * HD * heads

    def swap(array, axis):
        return lax.all_to_all(array, axis, 0, 0, tiled=True)

    whole = (length, width)
    block = pltpu.VMEM(whole, BF16)
    three = [block, block, block, pltpu.SemaphoreType.DMA((3,))]
    first, row = call(
        functools.partial(update_kernel, blocks),
        [like((blocks * (rows + 1), HD)), like((8, length))],
        log_decay,
        key_rows,
        values,
        flops=narrow,
        places_in={0: pltpu.HBM, 1: pltpu.HBM, 2: pltpu.HBM},
        scratch=[
            pltpu.VMEM(log_decay.shape, F32),
            pltpu.SemaphoreType.DMA,
            block,
            block,
            pltpu.SemaphoreType.DMA((2,)),
        ],
    )
    got = swap(first.reshape(blocks, rows + 1, 1, HD), "ctx").reshape(first.shape)
    local, column, gain, turned = call(
        local_kernel,
        [like(whole), like((length, HD)), like((8, width)), like((width, length), BF16)],
        queries,
        key_rows,
        values,
        row,
        gain,
        flops=2 * square,
        places_in={0: pltpu.HBM, 1: pltpu.HBM, 2: pltpu.HBM},
        places_out={3: pltpu.HBM},
        scratch=[*three, pltpu.VMEM((width, length), BF16), pltpu.SemaphoreType.DMA],
    )
    states, totals = call(
        forward_kernel,
        [like((blocks, rows, HD)), like((blocks, 8, HD))],
        got,
    )
    state_in = swap(states, "ctx")
    output, sums, low = call(
        output_kernel,
        [like(whole), like((groups, 2 * length // HD, HD)), like((heads * HD, HD), BF16)],
        queries,
        local,
        state_in,
        column,
        grad_normed,
        gain,
        flops=narrow,
    )
    sums = swap(sums, "head")
    grad, second = call(
        grad_kernel,
        [like(whole, BF16), like((blocks, rows, HD))],
        sums,
        output,
        grad_normed,
        gain,
        turned,
        flops=narrow,
    )
    got = swap(second, "ctx")
    (states,) = call(
        backward_kernel,
        [like((blocks, rows, HD))],
        got,
        totals,
    )
    state_out = swap(states, "ctx")
    grad_query, key_part, value_part = call(
        pull_kernel,
        [like(whole, BF16), like(whole), like(whole)],
        queries,
        key_rows,
        values,
        grad,
        low,
        row,
        flops=5 * square,
        places_in={0: pltpu.HBM, 1: pltpu.HBM, 2: pltpu.HBM},
        places_out={0: pltpu.HBM},
        scratch=[*three, block, pltpu.SemaphoreType.DMA((heads,))],
    )
    grad_key, grad_value = call(
        finish_kernel,
        [like(whole, BF16), like(whole, BF16)],
        key_part,
        value_part,
        key_rows,
        values,
        state_out,
        row,
        flops=2 * narrow,
        places_out={0: pltpu.HBM, 1: pltpu.HBM},
        scratch=[block, block, pltpu.SemaphoreType.DMA((2 * heads,))],
    )
    return grad_query, grad_key, grad_value


def solution(mesh):
    blocks, groups = mesh.shape["ctx"], mesh.shape["head"]

    def run(*arrays):
        return on_device(blocks, groups, *arrays)

    return jax.shard_map(
        run,
        mesh=mesh,
        in_specs=(
            P("ctx", "head"),
            P("ctx", "head"),
            P("ctx", "head"),
            P("head", "ctx"),
            P("head"),
            P("ctx", "head"),
        ),
        out_specs=(P("ctx", "head"), P("ctx", "head"), P("ctx", "head")),
        check_vma=False,
    )
```

```python
import functools

import jax
import jax.numpy as jnp
from jax import lax
from jax.experimental import pallas as pl
from jax.experimental.pallas import tpu as pltpu
from jax.sharding import PartitionSpec as P

HD = 128
EPSILON = 1e-05
F32 = jnp.float32
BF16 = jnp.bfloat16
VMEM_BYTES = 16 * 1024 * 1024


def dot(lhs, rhs, lhs_dim, rhs_dim):
    return lax.dot_general(
        lhs, rhs, (((lhs_dim,), (rhs_dim,)), ((), ())), preferred_element_type=F32
    )


def call(body, out_shapes, *operands, flops=0, places_in={}, places_out={}, scratch=()):
    moved = sum(a.size * a.dtype.itemsize for a in operands)
    moved += sum(s.size * s.dtype.itemsize for s in out_shapes)

    def specs(count, outside):
        return [
            pl.BlockSpec(memory_space=outside.get(i, pltpu.VMEM)) for i in range(count)
        ]

    operands = [
        pltpu.with_memory_space_constraint(a, places_in[i]) if i in places_in else a
        for i, a in enumerate(operands)
    ]
    return pl.pallas_call(
        body,
        out_shape=[
            places_out[i](s.shape, s.dtype) if i in places_out else s
            for i, s in enumerate(out_shapes)
        ],
        in_specs=specs(len(operands), places_in),
        out_specs=specs(len(out_shapes), places_out),
        scratch_shapes=scratch,
        compiler_params=pltpu.CompilerParams(vmem_limit_bytes=VMEM_BYTES),
        cost_estimate=pl.CostEstimate(flops=flops, bytes_accessed=moved, transcendentals=0),
    )(*operands)


def like(shape, dtype=F32):
    return jax.ShapeDtypeStruct(shape, dtype)


def head_columns(head):
    return slice(head * HD, (head + 1) * HD)


def turn(rows):
    return jnp.concatenate([rows, jnp.zeros((HD - 8, rows.shape[1]), F32)], axis=0).T


def down(pieces):
    return jnp.concatenate(
        [
            jnp.broadcast_to(pieces[i : i + 1], (HD, HD)).T
            for i in range(pieces.shape[0])
        ],
        axis=0,
    )


def cut(row):
    return jnp.concatenate(
        [row[:, head_columns(i)] for i in range(row.shape[1] // HD)], axis=0
    )


def tail_rows(row_ref):
    running = row_ref[...]
    return jnp.exp(running[:, running.shape[1] - 1 :] - running)


def load_all(sources, buffers, semaphores):
    loads = [
        pltpu.make_async_copy(source, buffer, semaphores.at[i])
        for i, (source, buffer) in enumerate(zip(sources, buffers))
    ]
    for load in loads:
        load.start()
    return loads


def update_kernel(
    targets,
    log_in,
    key_in,
    value_in,
    send_ref,
    row_ref,
    log_ref,
    log_semaphore,
    key_ref,
    value_ref,
    semaphores,
):
    load_logs = pltpu.make_async_copy(log_in, log_ref, log_semaphore)
    load_logs.start()
    loads = load_all((key_in, value_in), (key_ref, value_ref), semaphores)
    heads, length = log_ref.shape
    load_logs.wait()
    logs = jnp.concatenate([log_ref[...], jnp.zeros((8 - heads, length), F32)], axis=0)
    pieces = length // HD
    stacked = jnp.concatenate([logs[:, head_columns(i)] for i in range(pieces)], axis=0)
    high = stacked.astype(BF16)
    rest = stacked - high.astype(F32)
    middle = rest.astype(BF16)
    low = (rest - middle.astype(F32)).astype(BF16)
    before = lax.broadcasted_iota(jnp.int32, (HD, HD), 0)
    after = lax.broadcasted_iota(jnp.int32, (HD, HD), 1)
    upper = jnp.where(before <= after, 1.0, 0.0).astype(BF16)
    three = dot(jnp.concatenate([high, middle, low], axis=0), upper, 1, 0)
    count = 8 * pieces
    sums = (three[2 * count :] + three[count : 2 * count]) + three[:count]
    parts = []
    offset = jnp.zeros((8, 1), F32)
    for i in range(pieces):
        part = sums[i * 8 : (i + 1) * 8] + offset
        offset = part[:, HD - 1 : HD]
        parts.append(part)
    running = jnp.concatenate(parts, axis=1)
    row_ref[...] = running
    tail = jnp.exp(offset - running)
    per_head = targets // heads
    rows = heads * HD // targets
    for target in range(targets):
        last = target * (rows + 1) + rows
        head = target // per_head
        send_ref[last : last + 1] = jnp.broadcast_to(offset[head : head + 1], (1, HD))
    for load in loads:
        load.wait()
    for head in range(heads):
        turned = key_ref[:, head_columns(head)].T.astype(F32)
        scaled = (turned * tail[head : head + 1]).astype(BF16)
        update = dot(scaled, value_ref[:, head_columns(head)], 1, 0)
        for i in range(per_head):
            first = (head * per_head + i) * (rows + 1)
            send_ref[first : first + rows] = update[i * rows : (i + 1) * rows]


def forward_kernel(got_ref, send_ref, total_ref):
    blocks, rows = send_ref.shape[:2]
    state = jnp.zeros((rows, HD), F32)
    for block in range(blocks):
        first = block * (rows + 1)
        send_ref[block] = state
        total = got_ref[first + rows : first + rows + 1]
        total_ref[block] = jnp.broadcast_to(total, total_ref.shape[1:])
        state = jnp.exp(total) * state + got_ref[first : first + rows]


def backward_kernel(got_ref, total_ref, send_ref):
    blocks, rows = send_ref.shape[:2]
    factors = jnp.exp(total_ref[:, :1, :])
    state = jnp.zeros((rows, HD), F32)
    for block in reversed(range(blocks)):
        send_ref[block] = state
        state = factors[block] * state + got_ref[block]


def within_block(column, row, diagonal):
    spread = column - row
    if not diagonal:
        return jnp.exp(jnp.minimum(spread, 0.0))
    size = spread.shape[0]
    later = lax.broadcasted_iota(jnp.int32, (size, size), 0)
    earlier = lax.broadcasted_iota(jnp.int32, (size, size), 1)
    return jnp.where(later >= earlier, jnp.exp(jnp.minimum(spread, 0.0)), 0.0)


TILE = 256


def tiles(length):
    return [
        (slice(t, t + TILE), slice(j, j + TILE), t == j)
        for t in range(0, length, TILE)
        for j in range(0, t + TILE, TILE)
    ]


def local_kernel(
    query_in,
    key_in,
    value_in,
    row_ref,
    gain_in,
    local_ref,
    gain_ref,
    turned_out,
    query_ref,
    key_ref,
    value_ref,
    semaphores,
    turned_ref,
    store_semaphore,
):
    length = query_ref.shape[0]
    loads = load_all((query_in, key_in, value_in), (query_ref, key_ref, value_ref), semaphores)
    gain_ref[...] = jnp.broadcast_to(gain_in[...], gain_ref.shape)
    running = row_ref[...]
    columns = turn(running)
    for load in loads:
        load.wait()
    for head in range(query_ref.shape[1] // HD):
        cols = head_columns(head)
        grown = jnp.exp(running[head : head + 1])
        turned_ref[cols] = (query_ref[:, cols].T.astype(F32) * grown).astype(BF16)
    store = pltpu.make_async_copy(turned_ref, turned_out, store_semaphore)
    store.start()
    for head in range(query_ref.shape[1] // HD):
        cols = head_columns(head)
        sums = {}
        for t, j, diagonal in tiles(length):
            within = within_block(
                columns[t, head : head + 1], row_ref[head : head + 1, j], diagonal
            )
            scores = dot(query_ref[t, cols], key_ref[j, cols], 1, 1)
            masked = (scores * within).astype(BF16)
            part = dot(masked, value_ref[j, cols], 1, 0)
            sums[t.start] = sums[t.start] + part if t.start in sums else part
        for start, value in sums.items():
            local_ref[start : start + TILE, cols] = value
    store.wait()


def output_kernel(
    query_ref, local_ref, state_ref, row_ref, normed_ref, gain_ref, output_ref, send_ref, low_ref
):
    length = query_ref.shape[0]
    low_ref[...] = state_ref[...].reshape(low_ref.shape).astype(BF16)
    grown = jnp.exp(row_ref[...])
    squares = jnp.zeros((length, HD), F32)
    crosses = jnp.zeros((length, HD), F32)
    for head in range(query_ref.shape[1] // HD):
        cols = head_columns(head)
        carried = dot(query_ref[:, cols], low_ref[cols], 1, 0)
        output = local_ref[:, cols] + down(cut(grown[head : head + 1])) * carried
        output_ref[:, cols] = output
        gained = normed_ref[:, cols].astype(F32) * gain_ref[:1, cols]
        squares = squares + output * output
        crosses = crosses + output * gained
    sums = []
    for total in (squares, crosses):
        for i in range(length // HD):
            sums.append(jnp.sum(total[head_columns(i)].T, axis=0, keepdims=True))
    packed = jnp.concatenate(sums, axis=0)
    send_ref[...] = jnp.broadcast_to(packed[None], send_ref.shape)


def grad_kernel(sums_ref, output_ref, normed_ref, gain_ref, turned_ref, grad_ref, send_ref):
    length, width = output_ref.shape
    heads = width // HD
    pieces = length // HD
    channels = sums_ref.shape[0] * width
    sums = jnp.sum(sums_ref[...], axis=0)
    inverse = lax.rsqrt(sums[:pieces] / channels + EPSILON)
    inner = sums[pieces:] / channels
    scale = inverse * inverse * inverse * inner

    inverse, scale = down(inverse), down(scale)
    targets, rows = send_ref.shape[:2]
    per_head = targets // heads
    for head in range(heads):
        cols = head_columns(head)
        gained = normed_ref[:, cols].astype(F32) * gain_ref[:1, cols]
        grad = (inverse * gained - output_ref[:, cols] * scale).astype(BF16)
        grad_ref[:, cols] = grad
        send_ref[head * per_head : (head + 1) * per_head] = dot(
            turned_ref[cols], grad, 1, 0
        ).reshape(per_head, rows, HD)


def add(sums, where, part):
    sums[where] = sums[where] + part if where in sums else part


def pull_kernel(
    query_in,
    key_in,
    value_in,
    grad_in,
    low_ref,
    row_ref,
    grad_query_out,
    key_part_ref,
    value_part_ref,
    query_ref,
    key_ref,
    value_ref,
    grad_ref,
    semaphores,
    grad_query_ref,
    store_semaphores,
):
    length, width = query_ref.shape
    loads = load_all((query_in, key_in, value_in, grad_in,), (query_ref, key_ref, value_ref, grad_ref,), semaphores)
    columns, grown = turn(row_ref[...]), turn(jnp.exp(row_ref[...]))
    for load in loads:
        load.wait()
    stores = []
    for head in range(width // HD):
        cols = head_columns(head)
        query_sums, key_sums, value_sums = {}, {}, {}
        query_turned, grad_turned = query_ref[:, cols].T, grad_ref[:, cols].T
        for t, j, diagonal in tiles(length):
            within = within_block(columns[t, head : head + 1], row_ref[head : head + 1, j], diagonal)
            query, key, grad = query_ref[t, cols], key_ref[j, cols], grad_ref[t, cols]
            pulled = (dot(grad, value_ref[j, cols], 1, 1) * within).astype(BF16)
            masked = (dot(query, key, 1, 1) * within).astype(BF16)
            add(query_sums, t.start, dot(pulled, key, 1, 0))
            add(key_sums, j.start, dot(query_turned[:, t], pulled, 1, 0))
            add(value_sums, j.start, dot(grad_turned[:, t], masked, 1, 0))
        for start in range(0, length, TILE):
            here = slice(start, start + TILE)
            carried = dot(grad_ref[here, cols], low_ref[cols], 1, 1)
            grad_query_ref[here, cols] = (
                query_sums[start] + grown[here, head : head + 1] * carried
            ).astype(BF16)
        stores.append(
            pltpu.make_async_copy(
                grad_query_ref.at[:, cols], grad_query_out.at[:, cols], store_semaphores.at[head]
            )
        )
        stores[-1].start()
        for start in range(0, length, TILE):
            key_part_ref[start : start + TILE, cols] = key_sums[start].T
            value_part_ref[start : start + TILE, cols] = value_sums[start].T
    for store in stores:
        store.wait()


def finish_kernel(
    key_part_ref,
    value_part_ref,
    key_ref,
    value_ref,
    state_ref,
    row_ref,
    grad_key_out,
    grad_value_out,
    grad_key_ref,
    grad_value_ref,
    semaphores,
):
    low = state_ref[...].reshape(-1, HD).astype(BF16)
    stores = []
    tails = tail_rows(row_ref)
    for head in range(key_ref.shape[1] // HD):
        cols = head_columns(head)
        tail = down(cut(tails[head : head + 1]))
        grad_key_ref[:, cols] = (
            key_part_ref[:, cols] + tail * dot(value_ref[:, cols], low[cols], 1, 1)
        ).astype(BF16)
        grad_value_ref[:, cols] = (
            value_part_ref[:, cols] + tail * dot(key_ref[:, cols], low[cols], 1, 0)
        ).astype(BF16)
        for which, (source, target) in enumerate(
            ((grad_key_ref, grad_key_out), (grad_value_ref, grad_value_out))
        ):
            store = pltpu.make_async_copy(
                source.at[:, cols], target.at[:, cols], semaphores.at[2 * head + which]
            )
            store.start()
            stores.append(store)
    for store in stores:
        store.wait()


def on_device(blocks, groups, queries, key_rows, values, log_decay, norm_gain, grad_normed):
    length, width = queries.shape
    heads = log_decay.shape[0]
    rows = heads * HD // blocks
    gain = norm_gain.reshape(1, width)
    square = 2 * length * length * HD * heads
    narrow = 2 * length * HD * HD * heads

    def swap(array, axis):
        return lax.all_to_all(array, axis, 0, 0, tiled=True)

    whole = (length, width)
    block = pltpu.VMEM(whole, BF16)
    three = [block, block, block, pltpu.SemaphoreType.DMA((3,))]
    first, row = call(
        functools.partial(update_kernel, blocks),
        [like((blocks * (rows + 1), HD)), like((8, length))],
        log_decay,
        key_rows,
        values,
        flops=narrow,
        places_in={0: pltpu.HBM, 1: pltpu.HBM, 2: pltpu.HBM},
        scratch=[
            pltpu.VMEM(log_decay.shape, F32),
            pltpu.SemaphoreType.DMA,
            block,
            block,
            pltpu.SemaphoreType.DMA((2,)),
        ],
    )
    got = swap(first.reshape(blocks, rows + 1, 1, HD), "ctx").reshape(first.shape)
    local, gain, turned = call(
        local_kernel,
        [like(whole), like((8, width)), like((width, length), BF16)],
        queries,
        key_rows,
        values,
        row,
        gain,
        flops=2 * square,
        places_in={0: pltpu.HBM, 1: pltpu.HBM, 2: pltpu.HBM},
        places_out={2: pltpu.HBM},
        scratch=[*three, pltpu.VMEM((width, length), BF16), pltpu.SemaphoreType.DMA],
    )
    states, totals = call(
        forward_kernel,
        [like((blocks, rows, HD)), like((blocks, 8, HD))],
        got,
    )
    state_in = swap(states, "ctx")
    output, sums, low = call(
        output_kernel,
        [like(whole), like((groups, 2 * length // HD, HD)), like((heads * HD, HD), BF16)],
        queries,
        local,
        state_in,
        row,
        grad_normed,
        gain,
        flops=narrow,
    )
    sums = swap(sums, "head")
    grad, second = call(
        grad_kernel,
        [like(whole, BF16), like((blocks, rows, HD))],
        sums,
        output,
        grad_normed,
        gain,
        turned,
        flops=narrow,
    )
    got = swap(second, "ctx")
    (states,) = call(
        backward_kernel,
        [like((blocks, rows, HD))],
        got,
        totals,
    )
    state_out = swap(states, "ctx")
    grad_query, key_part, value_part = call(
        pull_kernel,
        [like(whole, BF16), like(whole), like(whole)],
        queries,
        key_rows,
        values,
        grad,
        low,
        row,
        flops=5 * square,
        places_in={i: pltpu.HBM for i in range(4)},
        places_out={0: pltpu.HBM},
        scratch=[
            *[block] * 4,
            pltpu.SemaphoreType.DMA((4,)),
            block,
            pltpu.SemaphoreType.DMA((heads,)),
        ],
    )
    grad_key, grad_value = call(
        finish_kernel,
        [like(whole, BF16), like(whole, BF16)],
        key_part,
        value_part,
        key_rows,
        values,
        state_out,
        row,
        flops=2 * narrow,
        places_out={0: pltpu.HBM, 1: pltpu.HBM},
        scratch=[block, block, pltpu.SemaphoreType.DMA((2 * heads,))],
    )
    return grad_query, grad_key, grad_value


def solution(mesh):
    blocks, groups = mesh.shape["ctx"], mesh.shape["head"]

    def run(*arrays):
        return on_device(blocks, groups, *arrays)

    return jax.shard_map(
        run,
        mesh=mesh,
        in_specs=(
            P("ctx", "head"),
            P("ctx", "head"),
            P("ctx", "head"),
            P("head", "ctx"),
            P("head"),
            P("ctx", "head"),
        ),
        out_specs=(P("ctx", "head"), P("ctx", "head"), P("ctx", "head")),
        check_vma=False,
    )
```

```python
import functools

import jax
import jax.numpy as jnp
from jax import lax
from jax.experimental import pallas as pl
from jax.experimental.pallas import tpu as pltpu
from jax.sharding import PartitionSpec as P

HD = 128
EPSILON = 1e-05
F32 = jnp.float32
BF16 = jnp.bfloat16
VMEM_BYTES = 16 * 1024 * 1024


def dot(lhs, rhs, lhs_dim, rhs_dim):
    return lax.dot_general(
        lhs, rhs, (((lhs_dim,), (rhs_dim,)), ((), ())), preferred_element_type=F32
    )


def call(body, out_shapes, *operands, flops=0, places_in={}, places_out={}, scratch=()):
    moved = sum(a.size * a.dtype.itemsize for a in operands)
    moved += sum(s.size * s.dtype.itemsize for s in out_shapes)

    def specs(count, outside):
        return [
            pl.BlockSpec(memory_space=outside.get(i, pltpu.VMEM)) for i in range(count)
        ]

    operands = [
        pltpu.with_memory_space_constraint(a, places_in[i]) if i in places_in else a
        for i, a in enumerate(operands)
    ]
    return pl.pallas_call(
        body,
        out_shape=[
            places_out[i](s.shape, s.dtype) if i in places_out else s
            for i, s in enumerate(out_shapes)
        ],
        in_specs=specs(len(operands), places_in),
        out_specs=specs(len(out_shapes), places_out),
        scratch_shapes=scratch,
        compiler_params=pltpu.CompilerParams(vmem_limit_bytes=VMEM_BYTES),
        cost_estimate=pl.CostEstimate(flops=flops, bytes_accessed=moved, transcendentals=0),
    )(*operands)


def like(shape, dtype=F32):
    return jax.ShapeDtypeStruct(shape, dtype)


def head_columns(head):
    return slice(head * HD, (head + 1) * HD)


def turn(rows):
    return jnp.concatenate([rows, jnp.zeros((HD - 8, rows.shape[1]), F32)], axis=0).T


def down(pieces):
    return jnp.concatenate(
        [
            jnp.broadcast_to(pieces[i : i + 1], (HD, HD)).T
            for i in range(pieces.shape[0])
        ],
        axis=0,
    )


def cut(row):
    return jnp.concatenate(
        [row[:, head_columns(i)] for i in range(row.shape[1] // HD)], axis=0
    )


def tail_rows(row_ref):
    running = row_ref[...]
    return jnp.exp(running[:, running.shape[1] - 1 :] - running)


def load_all(sources, buffers, semaphores):
    loads = [
        pltpu.make_async_copy(source, buffer, semaphores.at[i])
        for i, (source, buffer) in enumerate(zip(sources, buffers))
    ]
    for load in loads:
        load.start()
    return loads


def update_kernel(
    targets,
    log_in,
    key_in,
    value_in,
    send_ref,
    row_ref,
    log_ref,
    log_semaphore,
    key_ref,
    value_ref,
    semaphores,
):
    load_logs = pltpu.make_async_copy(log_in, log_ref, log_semaphore)
    load_logs.start()
    loads = load_all((key_in, value_in), (key_ref, value_ref), semaphores)
    heads, length = log_ref.shape
    load_logs.wait()
    logs = jnp.concatenate([log_ref[...], jnp.zeros((8 - heads, length), F32)], axis=0)
    pieces = length // HD
    stacked = jnp.concatenate([logs[:, head_columns(i)] for i in range(pieces)], axis=0)
    high = stacked.astype(BF16)
    rest = stacked - high.astype(F32)
    middle = rest.astype(BF16)
    low = (rest - middle.astype(F32)).astype(BF16)
    before = lax.broadcasted_iota(jnp.int32, (HD, HD), 0)
    after = lax.broadcasted_iota(jnp.int32, (HD, HD), 1)
    upper = jnp.where(before <= after, 1.0, 0.0).astype(BF16)
    three = dot(jnp.concatenate([high, middle, low], axis=0), upper, 1, 0)
    count = 8 * pieces
    sums = (three[2 * count :] + three[count : 2 * count]) + three[:count]
    parts = []
    offset = jnp.zeros((8, 1), F32)
    for i in range(pieces):
        part = sums[i * 8 : (i + 1) * 8] + offset
        offset = part[:, HD - 1 : HD]
        parts.append(part)
    running = jnp.concatenate(parts, axis=1)
    row_ref[...] = running
    tail = jnp.exp(offset - running)
    per_head = targets // heads
    rows = heads * HD // targets
    for target in range(targets):
        last = target * (rows + 1) + rows
        head = target // per_head
        send_ref[last : last + 1] = jnp.broadcast_to(offset[head : head + 1], (1, HD))
    for load in loads:
        load.wait()
    for head in range(heads):
        turned = key_ref[:, head_columns(head)].T.astype(F32)
        scaled = (turned * tail[head : head + 1]).astype(BF16)
        update = dot(scaled, value_ref[:, head_columns(head)], 1, 0)
        for i in range(per_head):
            first = (head * per_head + i) * (rows + 1)
            send_ref[first : first + rows] = update[i * rows : (i + 1) * rows]


def exchange_order(blocks):
    if blocks != 32:
        return tuple(reversed(range(blocks)))
    order = []
    for block in reversed(range(0, blocks, 2)):
        x, y, core = block // 8, block // 2 % 4, block % 2
        order += [((x + 2) % 4 * 4 + (y + 2) % 4) * 2 + 1 - core, block]
    return tuple(order)


def forward_kernel(order, got_ref, send_ref, total_ref):
    rows = send_ref.shape[1]
    state = jnp.zeros((rows, HD), F32)
    for block in (order.index(i) for i in range(len(order))):
        first = block * (rows + 1)
        send_ref[block] = state
        total = got_ref[first + rows : first + rows + 1]
        total_ref[block] = jnp.broadcast_to(total, total_ref.shape[1:])
        state = jnp.exp(total) * state + got_ref[first : first + rows]


def backward_kernel(order, got_ref, total_ref, send_ref):
    rows = send_ref.shape[1]
    factors = jnp.exp(total_ref[:, :1, :])
    state = jnp.zeros((rows, HD), F32)
    for block in (order.index(i) for i in reversed(range(len(order)))):
        send_ref[block] = state
        state = factors[block] * state + got_ref[block]


def within_block(column, row, diagonal):
    spread = column - row
    if not diagonal:
        return jnp.exp(jnp.minimum(spread, 0.0))
    size = spread.shape[0]
    later = lax.broadcasted_iota(jnp.int32, (size, size), 0)
    earlier = lax.broadcasted_iota(jnp.int32, (size, size), 1)
    return jnp.where(later >= earlier, jnp.exp(jnp.minimum(spread, 0.0)), 0.0)


TILE = 256


def tiles(length):
    return [
        (slice(t, t + TILE), slice(j, j + TILE), t == j)
        for t in range(0, length, TILE)
        for j in range(0, t + TILE, TILE)
    ]


def local_kernel(
    query_in,
    key_in,
    value_in,
    row_ref,
    gain_in,
    local_ref,
    gain_ref,
    turned_out,
    query_ref,
    key_ref,
    value_ref,
    semaphores,
    turned_ref,
    store_semaphore,
):
    length = query_ref.shape[0]
    loads = load_all((query_in, key_in, value_in), (query_ref, key_ref, value_ref), semaphores)
    gain_ref[...] = jnp.broadcast_to(gain_in[...], gain_ref.shape)
    running = row_ref[...]
    columns = turn(running)
    for load in loads:
        load.wait()
    for head in range(query_ref.shape[1] // HD):
        cols = head_columns(head)
        grown = jnp.exp(running[head : head + 1])
        turned_ref[cols] = (query_ref[:, cols].T.astype(F32) * grown).astype(BF16)
    store = pltpu.make_async_copy(turned_ref, turned_out, store_semaphore)
    store.start()
    for head in range(query_ref.shape[1] // HD):
        cols = head_columns(head)
        sums = {}
        for t, j, diagonal in tiles(length):
            within = within_block(
                columns[t, head : head + 1], row_ref[head : head + 1, j], diagonal
            )
            scores = dot(query_ref[t, cols], key_ref[j, cols], 1, 1)
            masked = (scores * within).astype(BF16)
            part = dot(masked, value_ref[j, cols], 1, 0)
            sums[t.start] = sums[t.start] + part if t.start in sums else part
        for start, value in sums.items():
            local_ref[start : start + TILE, cols] = value
    store.wait()


def output_kernel(
    query_ref, local_ref, state_ref, row_ref, normed_ref, gain_ref, output_ref, send_ref, low_ref
):
    length = query_ref.shape[0]
    low_ref[...] = state_ref[...].reshape(low_ref.shape).astype(BF16)
    grown = jnp.exp(row_ref[...])
    squares = jnp.zeros((length, HD), F32)
    crosses = jnp.zeros((length, HD), F32)
    for head in range(query_ref.shape[1] // HD):
        cols = head_columns(head)
        carried = dot(query_ref[:, cols], low_ref[cols], 1, 0)
        output = local_ref[:, cols] + down(cut(grown[head : head + 1])) * carried
        output_ref[:, cols] = output
        gained = normed_ref[:, cols].astype(F32) * gain_ref[:1, cols]
        squares = squares + output * output
        crosses = crosses + output * gained
    sums = []
    for total in (squares, crosses):
        for i in range(length // HD):
            sums.append(jnp.sum(total[head_columns(i)].T, axis=0, keepdims=True))
    packed = jnp.concatenate(sums, axis=0)
    send_ref[...] = jnp.broadcast_to(packed[None], send_ref.shape)


def grad_kernel(sums_ref, output_ref, normed_ref, gain_ref, turned_ref, grad_ref, send_ref):
    length, width = output_ref.shape
    heads = width // HD
    pieces = length // HD
    channels = sums_ref.shape[0] * width
    sums = jnp.sum(sums_ref[...], axis=0)
    inverse = lax.rsqrt(sums[:pieces] / channels + EPSILON)
    inner = sums[pieces:] / channels
    scale = inverse * inverse * inverse * inner

    inverse, scale = down(inverse), down(scale)
    targets, rows = send_ref.shape[:2]
    per_head = targets // heads
    for head in range(heads):
        cols = head_columns(head)
        gained = normed_ref[:, cols].astype(F32) * gain_ref[:1, cols]
        grad = (inverse * gained - output_ref[:, cols] * scale).astype(BF16)
        grad_ref[:, cols] = grad
        send_ref[head * per_head : (head + 1) * per_head] = dot(
            turned_ref[cols], grad, 1, 0
        ).reshape(per_head, rows, HD)


def add(sums, where, part):
    sums[where] = sums[where] + part if where in sums else part


def pull_kernel(
    query_in,
    key_in,
    value_in,
    grad_in,
    low_ref,
    row_ref,
    grad_query_out,
    key_part_ref,
    value_part_ref,
    query_ref,
    key_ref,
    value_ref,
    grad_ref,
    semaphores,
    grad_query_ref,
    store_semaphores,
):
    length, width = query_ref.shape
    loads = load_all((query_in, key_in, value_in, grad_in,), (query_ref, key_ref, value_ref, grad_ref,), semaphores)
    columns, grown = turn(row_ref[...]), turn(jnp.exp(row_ref[...]))
    for load in loads:
        load.wait()
    stores = []
    for head in range(width // HD):
        cols = head_columns(head)
        query_sums, key_sums, value_sums = {}, {}, {}
        query_turned, grad_turned = query_ref[:, cols].T, grad_ref[:, cols].T
        for t, j, diagonal in tiles(length):
            within = within_block(columns[t, head : head + 1], row_ref[head : head + 1, j], diagonal)
            query, key, grad = query_ref[t, cols], key_ref[j, cols], grad_ref[t, cols]
            pulled = (dot(grad, value_ref[j, cols], 1, 1) * within).astype(BF16)
            masked = (dot(query, key, 1, 1) * within).astype(BF16)
            add(query_sums, t.start, dot(pulled, key, 1, 0))
            add(key_sums, j.start, dot(query_turned[:, t], pulled, 1, 0))
            add(value_sums, j.start, dot(grad_turned[:, t], masked, 1, 0))
        for start in range(0, length, TILE):
            here = slice(start, start + TILE)
            carried = dot(grad_ref[here, cols], low_ref[cols], 1, 1)
            grad_query_ref[here, cols] = (
                query_sums[start] + grown[here, head : head + 1] * carried
            ).astype(BF16)
        stores.append(
            pltpu.make_async_copy(
                grad_query_ref.at[:, cols], grad_query_out.at[:, cols], store_semaphores.at[head]
            )
        )
        stores[-1].start()
        for start in range(0, length, TILE):
            key_part_ref[start : start + TILE, cols] = key_sums[start].T
            value_part_ref[start : start + TILE, cols] = value_sums[start].T
    for store in stores:
        store.wait()


def finish_kernel(
    key_part_ref,
    value_part_ref,
    key_ref,
    value_ref,
    state_ref,
    row_ref,
    grad_key_out,
    grad_value_out,
    grad_key_ref,
    grad_value_ref,
    semaphores,
):
    low = state_ref[...].reshape(-1, HD).astype(BF16)
    stores = []
    tails = tail_rows(row_ref)
    for head in range(key_ref.shape[1] // HD):
        cols = head_columns(head)
        tail = down(cut(tails[head : head + 1]))
        grad_key_ref[:, cols] = (
            key_part_ref[:, cols] + tail * dot(value_ref[:, cols], low[cols], 1, 1)
        ).astype(BF16)
        grad_value_ref[:, cols] = (
            value_part_ref[:, cols] + tail * dot(key_ref[:, cols], low[cols], 1, 0)
        ).astype(BF16)
        for which, (source, target) in enumerate(
            ((grad_key_ref, grad_key_out), (grad_value_ref, grad_value_out))
        ):
            store = pltpu.make_async_copy(
                source.at[:, cols], target.at[:, cols], semaphores.at[2 * head + which]
            )
            store.start()
            stores.append(store)
    for store in stores:
        store.wait()


def on_device(blocks, groups, queries, key_rows, values, log_decay, norm_gain, grad_normed):
    length, width = queries.shape
    heads = log_decay.shape[0]
    rows = heads * HD // blocks
    gain = norm_gain.reshape(1, width)
    square = 2 * length * length * HD * heads
    narrow = 2 * length * HD * HD * heads

    order = exchange_order(blocks)

    def swap(array, axis):
        groups = [list(order)] if axis == "ctx" else None
        return lax.all_to_all(array, axis, 0, 0, axis_index_groups=groups, tiled=True)

    whole = (length, width)
    block = pltpu.VMEM(whole, BF16)
    three = [block, block, block, pltpu.SemaphoreType.DMA((3,))]
    first, row = call(
        functools.partial(update_kernel, blocks),
        [like((blocks * (rows + 1), HD)), like((8, length))],
        log_decay,
        key_rows,
        values,
        flops=narrow,
        places_in={0: pltpu.HBM, 1: pltpu.HBM, 2: pltpu.HBM},
        scratch=[
            pltpu.VMEM(log_decay.shape, F32),
            pltpu.SemaphoreType.DMA,
            block,
            block,
            pltpu.SemaphoreType.DMA((2,)),
        ],
    )
    got = swap(first.reshape(blocks, rows + 1, 1, HD), "ctx").reshape(first.shape)
    local, gain, turned = call(
        local_kernel,
        [like(whole), like((8, width)), like((width, length), BF16)],
        queries,
        key_rows,
        values,
        row,
        gain,
        flops=2 * square,
        places_in={0: pltpu.HBM, 1: pltpu.HBM, 2: pltpu.HBM},
        places_out={2: pltpu.HBM},
        scratch=[*three, pltpu.VMEM((width, length), BF16), pltpu.SemaphoreType.DMA],
    )
    states, totals = call(
        functools.partial(forward_kernel, order),
        [like((blocks, rows, HD)), like((blocks, 8, HD))],
        got,
    )
    state_in = swap(states, "ctx")
    output, sums, low = call(
        output_kernel,
        [like(whole), like((groups, 2 * length // HD, HD)), like((heads * HD, HD), BF16)],
        queries,
        local,
        state_in,
        row,
        grad_normed,
        gain,
        flops=narrow,
    )
    sums = swap(sums, "head")
    grad, second = call(
        grad_kernel,
        [like(whole, BF16), like((blocks, rows, HD))],
        sums,
        output,
        grad_normed,
        gain,
        turned,
        flops=narrow,
    )
    got = swap(second, "ctx")
    (states,) = call(
        functools.partial(backward_kernel, order),
        [like((blocks, rows, HD))],
        got,
        totals,
    )
    state_out = swap(states, "ctx")
    grad_query, key_part, value_part = call(
        pull_kernel,
        [like(whole, BF16), like(whole), like(whole)],
        queries,
        key_rows,
        values,
        grad,
        low,
        row,
        flops=5 * square,
        places_in={i: pltpu.HBM for i in range(4)},
        places_out={0: pltpu.HBM},
        scratch=[
            *[block] * 4,
            pltpu.SemaphoreType.DMA((4,)),
            block,
            pltpu.SemaphoreType.DMA((heads,)),
        ],
    )
    grad_key, grad_value = call(
        finish_kernel,
        [like(whole, BF16), like(whole, BF16)],
        key_part,
        value_part,
        key_rows,
        values,
        state_out,
        row,
        flops=2 * narrow,
        places_out={0: pltpu.HBM, 1: pltpu.HBM},
        scratch=[block, block, pltpu.SemaphoreType.DMA((2 * heads,))],
    )
    return grad_query, grad_key, grad_value


def solution(mesh):
    blocks, groups = mesh.shape["ctx"], mesh.shape["head"]

    def run(*arrays):
        return on_device(blocks, groups, *arrays)

    return jax.shard_map(
        run,
        mesh=mesh,
        in_specs=(
            P("ctx", "head"),
            P("ctx", "head"),
            P("ctx", "head"),
            P("head", "ctx"),
            P("head"),
            P("ctx", "head"),
        ),
        out_specs=(P("ctx", "head"), P("ctx", "head"), P("ctx", "head")),
        check_vma=False,
    )
```

```python
import functools

import jax
import jax.numpy as jnp
from jax import lax
from jax.experimental import pallas as pl
from jax.experimental.pallas import tpu as pltpu
from jax.sharding import PartitionSpec as P

HD = 128
EPSILON = 1e-05
F32 = jnp.float32
BF16 = jnp.bfloat16
VMEM_BYTES = 16 * 1024 * 1024


def dot(lhs, rhs, lhs_dim, rhs_dim):
    return lax.dot_general(
        lhs, rhs, (((lhs_dim,), (rhs_dim,)), ((), ())), preferred_element_type=F32
    )


def call(body, out_shapes, *operands, flops=0, places_in={}, places_out={}, scratch=()):
    moved = sum(a.size * a.dtype.itemsize for a in operands)
    moved += sum(s.size * s.dtype.itemsize for s in out_shapes)

    def specs(count, outside):
        return [
            pl.BlockSpec(memory_space=outside.get(i, pltpu.VMEM)) for i in range(count)
        ]

    operands = [
        pltpu.with_memory_space_constraint(a, places_in[i]) if i in places_in else a
        for i, a in enumerate(operands)
    ]
    return pl.pallas_call(
        body,
        out_shape=[
            places_out[i](s.shape, s.dtype) if i in places_out else s
            for i, s in enumerate(out_shapes)
        ],
        in_specs=specs(len(operands), places_in),
        out_specs=specs(len(out_shapes), places_out),
        scratch_shapes=scratch,
        compiler_params=pltpu.CompilerParams(vmem_limit_bytes=VMEM_BYTES),
        cost_estimate=pl.CostEstimate(flops=flops, bytes_accessed=moved, transcendentals=0),
    )(*operands)


def like(shape, dtype=F32):
    return jax.ShapeDtypeStruct(shape, dtype)


def head_columns(head):
    return slice(head * HD, (head + 1) * HD)


def turn(rows):
    return jnp.concatenate([rows, jnp.zeros((HD - 8, rows.shape[1]), F32)], axis=0).T


def down(pieces):
    return jnp.concatenate(
        [
            jnp.broadcast_to(pieces[i : i + 1], (HD, HD)).T
            for i in range(pieces.shape[0])
        ],
        axis=0,
    )


def cut(row):
    return jnp.concatenate(
        [row[:, head_columns(i)] for i in range(row.shape[1] // HD)], axis=0
    )


def tail_rows(row_ref):
    running = row_ref[...]
    return jnp.exp(running[:, running.shape[1] - 1 :] - running)


def load_all(sources, buffers, semaphores):
    loads = [
        pltpu.make_async_copy(source, buffer, semaphores.at[i])
        for i, (source, buffer) in enumerate(zip(sources, buffers))
    ]
    for load in loads:
        load.start()
    return loads


def update_kernel(
    targets,
    log_in,
    key_in,
    value_in,
    send_ref,
    row_ref,
    log_ref,
    log_semaphore,
    key_ref,
    value_ref,
    semaphores,
):
    load_logs = pltpu.make_async_copy(log_in, log_ref, log_semaphore)
    load_logs.start()
    loads = load_all((key_in, value_in), (key_ref, value_ref), semaphores)
    heads, length = log_ref.shape
    load_logs.wait()
    logs = jnp.concatenate([log_ref[...], jnp.zeros((8 - heads, length), F32)], axis=0)
    pieces = length // HD
    stacked = jnp.concatenate([logs[:, head_columns(i)] for i in range(pieces)], axis=0)
    high = stacked.astype(BF16)
    rest = stacked - high.astype(F32)
    middle = rest.astype(BF16)
    low = (rest - middle.astype(F32)).astype(BF16)
    before = lax.broadcasted_iota(jnp.int32, (HD, HD), 0)
    after = lax.broadcasted_iota(jnp.int32, (HD, HD), 1)
    upper = jnp.where(before <= after, 1.0, 0.0).astype(BF16)
    three = dot(jnp.concatenate([high, middle, low], axis=0), upper, 1, 0)
    count = 8 * pieces
    sums = (three[2 * count :] + three[count : 2 * count]) + three[:count]
    parts = []
    offset = jnp.zeros((8, 1), F32)
    for i in range(pieces):
        part = sums[i * 8 : (i + 1) * 8] + offset
        offset = part[:, HD - 1 : HD]
        parts.append(part)
    running = jnp.concatenate(parts, axis=1)
    row_ref[...] = running
    tail = jnp.exp(offset - running)
    per_head = targets // heads
    rows = heads * HD // targets
    for target in range(targets):
        last = target * (rows + 1) + rows
        head = target // per_head
        send_ref[last : last + 1] = jnp.broadcast_to(offset[head : head + 1], (1, HD))
    for load in loads:
        load.wait()
    for head in range(heads):
        turned = key_ref[:, head_columns(head)].T.astype(F32)
        scaled = (turned * tail[head : head + 1]).astype(BF16)
        update = dot(scaled, value_ref[:, head_columns(head)], 1, 0)
        for i in range(per_head):
            first = (head * per_head + i) * (rows + 1)
            send_ref[first : first + rows] = update[i * rows : (i + 1) * rows]


def exchange_order(blocks):
    if blocks != 32:
        return tuple(reversed(range(blocks)))
    order = []
    for block in reversed(range(0, blocks, 2)):
        x, y, core = block // 8, block // 2 % 4, block % 2
        order += [((x + 2) % 4 * 4 + (y + 2) % 4) * 2 + 1 - core, block]
    return tuple(order)


def forward_kernel(order, got_ref, send_ref, total_ref):
    rows = send_ref.shape[1]
    state = jnp.zeros((rows, HD), F32)
    for block in (order.index(i) for i in range(len(order))):
        first = block * (rows + 1)
        send_ref[block] = state
        total = got_ref[first + rows : first + rows + 1]
        total_ref[block] = jnp.broadcast_to(total, total_ref.shape[1:])
        state = jnp.exp(total) * state + got_ref[first : first + rows]


def backward_kernel(order, got_ref, total_ref, send_ref):
    rows = send_ref.shape[1]
    factors = jnp.exp(total_ref[:, :1, :])
    state = jnp.zeros((rows, HD), F32)
    for block in (order.index(i) for i in reversed(range(len(order)))):
        send_ref[block] = state
        state = factors[block] * state + got_ref[block]


def within_block(column, row, diagonal):
    spread = column - row
    if not diagonal:
        return jnp.exp(jnp.minimum(spread, 0.0))
    size = spread.shape[0]
    later = lax.broadcasted_iota(jnp.int32, (size, size), 0)
    earlier = lax.broadcasted_iota(jnp.int32, (size, size), 1)
    return jnp.where(later >= earlier, jnp.exp(jnp.minimum(spread, 0.0)), 0.0)


TILE = 256


def tiles(length):
    return [
        (slice(t, t + TILE), slice(j, j + TILE), t == j)
        for t in range(0, length, TILE)
        for j in range(0, t + TILE, TILE)
    ]


def local_kernel(
    query_in,
    key_in,
    value_in,
    row_ref,
    gain_in,
    local_ref,
    gain_ref,
    turned_out,
    query_ref,
    key_ref,
    value_ref,
    semaphores,
    turned_ref,
    store_semaphore,
):
    length = query_ref.shape[0]
    loads = load_all((query_in, key_in, value_in), (query_ref, key_ref, value_ref), semaphores)
    gain_ref[...] = jnp.broadcast_to(gain_in[...], gain_ref.shape)
    running = row_ref[...]
    columns = turn(running)
    for load in loads:
        load.wait()
    for head in range(query_ref.shape[1] // HD):
        cols = head_columns(head)
        grown = jnp.exp(running[head : head + 1])
        turned_ref[cols] = (query_ref[:, cols].T.astype(F32) * grown).astype(BF16)
    store = pltpu.make_async_copy(turned_ref, turned_out, store_semaphore)
    store.start()
    for head in range(query_ref.shape[1] // HD):
        cols = head_columns(head)
        sums = {}
        for t, j, diagonal in tiles(length):
            within = within_block(
                columns[t, head : head + 1], row_ref[head : head + 1, j], diagonal
            )
            scores = dot(query_ref[t, cols], key_ref[j, cols], 1, 1)
            masked = (scores * within).astype(BF16)
            part = dot(masked, value_ref[j, cols], 1, 0)
            sums[t.start] = sums[t.start] + part if t.start in sums else part
        for start, value in sums.items():
            local_ref[start : start + TILE, cols] = value
    store.wait()


def output_kernel(
    query_ref, local_ref, state_ref, row_ref, normed_ref, gain_ref, output_ref, send_ref, low_ref
):
    length = query_ref.shape[0]
    low_ref[...] = state_ref[...].reshape(low_ref.shape).astype(BF16)
    grown = jnp.exp(row_ref[...])
    squares = jnp.zeros((length, HD), F32)
    crosses = jnp.zeros((length, HD), F32)
    for head in range(query_ref.shape[1] // HD):
        cols = head_columns(head)
        carried = dot(query_ref[:, cols], low_ref[cols], 1, 0)
        output = local_ref[:, cols] + down(cut(grown[head : head + 1])) * carried
        output_ref[:, cols] = output
        gained = normed_ref[:, cols].astype(F32) * gain_ref[:1, cols]
        squares = squares + output * output
        crosses = crosses + output * gained
    sums = []
    for total in (squares, crosses):
        for i in range(length // HD):
            sums.append(jnp.sum(total[head_columns(i)].T, axis=0, keepdims=True))
    packed = jnp.concatenate(sums, axis=0)
    send_ref[...] = jnp.broadcast_to(packed[None], send_ref.shape)


def grad_kernel(sums_ref, output_ref, normed_ref, gain_ref, turned_ref, grad_ref, send_ref):
    length, width = output_ref.shape
    heads = width // HD
    pieces = length // HD
    channels = sums_ref.shape[0] * width
    sums = jnp.sum(sums_ref[...], axis=0)
    inverse = lax.rsqrt(sums[:pieces] / channels + EPSILON)
    inner = sums[pieces:] / channels
    scale = inverse * inverse * inverse * inner

    inverse, scale = down(inverse), down(scale)
    targets, rows = send_ref.shape[:2]
    per_head = targets // heads
    for head in range(heads):
        cols = head_columns(head)
        gained = normed_ref[:, cols].astype(F32) * gain_ref[:1, cols]
        grad = (inverse * gained - output_ref[:, cols] * scale).astype(BF16)
        grad_ref[:, cols] = grad
        send_ref[head * per_head : (head + 1) * per_head] = dot(
            turned_ref[cols], grad, 1, 0
        ).reshape(per_head, rows, HD)


def add(sums, where, part):
    sums[where] = sums[where] + part if where in sums else part


def pull_kernel(
    query_in,
    key_in,
    value_in,
    grad_in,
    low_ref,
    row_ref,
    grad_query_out,
    key_part_ref,
    value_part_ref,
    query_ref,
    key_ref,
    value_ref,
    grad_ref,
    semaphores,
    grad_query_ref,
    store_semaphores,
):
    length, width = query_ref.shape
    loads = load_all((query_in, key_in, value_in, grad_in,), (query_ref, key_ref, value_ref, grad_ref,), semaphores)
    columns, grown = turn(row_ref[...]), turn(jnp.exp(row_ref[...]))
    for load in loads:
        load.wait()
    stores = []
    for head in range(width // HD):
        cols = head_columns(head)
        query_sums, key_sums, value_sums = {}, {}, {}
        query_turned, grad_turned = query_ref[:, cols].T, grad_ref[:, cols].T
        for t, j, diagonal in tiles(length):
            within = within_block(columns[t, head : head + 1], row_ref[head : head + 1, j], diagonal)
            query, key, grad = query_ref[t, cols], key_ref[j, cols], grad_ref[t, cols]
            pulled = (dot(grad, value_ref[j, cols], 1, 1) * within).astype(BF16)
            masked = (dot(query, key, 1, 1) * within).astype(BF16)
            add(query_sums, t.start, dot(pulled, key, 1, 0))
            add(key_sums, j.start, dot(query_turned[:, t], pulled, 1, 0))
            add(value_sums, j.start, dot(grad_turned[:, t], masked, 1, 0))
        for start in range(0, length, TILE):
            here = slice(start, start + TILE)
            carried = dot(grad_ref[here, cols], low_ref[cols], 1, 1)
            grad_query_ref[here, cols] = (
                query_sums[start] + grown[here, head : head + 1] * carried
            ).astype(BF16)
        stores.append(
            pltpu.make_async_copy(
                grad_query_ref.at[:, cols], grad_query_out.at[:, cols], store_semaphores.at[head]
            )
        )
        stores[-1].start()
        for start in range(0, length, TILE):
            key_part_ref[start : start + TILE, cols] = key_sums[start].T
            value_part_ref[start : start + TILE, cols] = value_sums[start].T
    for store in stores:
        store.wait()


def finish_kernel(
    key_part_ref,
    value_part_ref,
    key_ref,
    value_ref,
    state_ref,
    row_ref,
    grad_key_out,
    grad_value_out,
    grad_key_ref,
    grad_value_ref,
    semaphores,
):
    low = state_ref[...].reshape(-1, HD).astype(BF16)
    stores = []
    tails = tail_rows(row_ref)
    for head in range(key_ref.shape[1] // HD):
        cols = head_columns(head)
        tail = down(cut(tails[head : head + 1]))
        grad_key_ref[:, cols] = (
            key_part_ref[:, cols] + tail * dot(value_ref[:, cols], low[cols], 1, 1)
        ).astype(BF16)
        grad_value_ref[:, cols] = (
            value_part_ref[:, cols] + tail * dot(key_ref[:, cols], low[cols], 1, 0)
        ).astype(BF16)
        for which, (source, target) in enumerate(
            ((grad_key_ref, grad_key_out), (grad_value_ref, grad_value_out))
        ):
            store = pltpu.make_async_copy(
                source.at[:, cols], target.at[:, cols], semaphores.at[2 * head + which]
            )
            store.start()
            stores.append(store)
    for store in stores:
        store.wait()


def on_device(blocks, groups, queries, key_rows, values, log_decay, norm_gain, grad_normed):
    length, width = queries.shape
    heads = log_decay.shape[0]
    rows = heads * HD // blocks
    gain = norm_gain.reshape(1, width)
    square = 2 * length * length * HD * heads
    narrow = 2 * length * HD * HD * heads

    order = exchange_order(blocks)

    def swap(array, axis):
        members = list(order) if axis == "ctx" else [7 * i % groups for i in range(groups)][::-1]
        return lax.all_to_all(array, axis, 0, 0, axis_index_groups=[members], tiled=True)

    whole = (length, width)
    block = pltpu.VMEM(whole, BF16)
    three = [block, block, block, pltpu.SemaphoreType.DMA((3,))]
    first, row = call(
        functools.partial(update_kernel, blocks),
        [like((blocks * (rows + 1), HD)), like((8, length))],
        log_decay,
        key_rows,
        values,
        flops=narrow,
        places_in={0: pltpu.HBM, 1: pltpu.HBM, 2: pltpu.HBM},
        scratch=[
            pltpu.VMEM(log_decay.shape, F32),
            pltpu.SemaphoreType.DMA,
            block,
            block,
            pltpu.SemaphoreType.DMA((2,)),
        ],
    )
    got = swap(first.reshape(blocks, rows + 1, 1, HD), "ctx").reshape(first.shape)
    local, gain, turned = call(
        local_kernel,
        [like(whole), like((8, width)), like((width, length), BF16)],
        queries,
        key_rows,
        values,
        row,
        gain,
        flops=2 * square,
        places_in={0: pltpu.HBM, 1: pltpu.HBM, 2: pltpu.HBM},
        places_out={2: pltpu.HBM},
        scratch=[*three, pltpu.VMEM((width, length), BF16), pltpu.SemaphoreType.DMA],
    )
    states, totals = call(
        functools.partial(forward_kernel, order),
        [like((blocks, rows, HD)), like((blocks, 8, HD))],
        got,
    )
    state_in = swap(states, "ctx")
    output, sums, low = call(
        output_kernel,
        [like(whole), like((groups, 2 * length // HD, HD)), like((heads * HD, HD), BF16)],
        queries,
        local,
        state_in,
        row,
        grad_normed,
        gain,
        flops=narrow,
    )
    sums = swap(sums, "head")
    grad, second = call(
        grad_kernel,
        [like(whole, BF16), like((blocks, rows, HD))],
        sums,
        output,
        grad_normed,
        gain,
        turned,
        flops=narrow,
    )
    got = swap(second, "ctx")
    (states,) = call(
        functools.partial(backward_kernel, order),
        [like((blocks, rows, HD))],
        got,
        totals,
    )
    state_out = swap(states, "ctx")
    grad_query, key_part, value_part = call(
        pull_kernel,
        [like(whole, BF16), like(whole), like(whole)],
        queries,
        key_rows,
        values,
        grad,
        low,
        row,
        flops=5 * square,
        places_in={i: pltpu.HBM for i in range(4)},
        places_out={0: pltpu.HBM},
        scratch=[
            *[block] * 4,
            pltpu.SemaphoreType.DMA((4,)),
            block,
            pltpu.SemaphoreType.DMA((heads,)),
        ],
    )
    grad_key, grad_value = call(
        finish_kernel,
        [like(whole, BF16), like(whole, BF16)],
        key_part,
        value_part,
        key_rows,
        values,
        state_out,
        row,
        flops=2 * narrow,
        places_out={0: pltpu.HBM, 1: pltpu.HBM},
        scratch=[block, block, pltpu.SemaphoreType.DMA((2 * heads,))],
    )
    return grad_query, grad_key, grad_value


def solution(mesh):
    blocks, groups = mesh.shape["ctx"], mesh.shape["head"]

    def run(*arrays):
        return on_device(blocks, groups, *arrays)

    return jax.shard_map(
        run,
        mesh=mesh,
        in_specs=(
            P("ctx", "head"),
            P("ctx", "head"),
            P("ctx", "head"),
            P("head", "ctx"),
            P("head"),
            P("ctx", "head"),
        ),
        out_specs=(P("ctx", "head"), P("ctx", "head"), P("ctx", "head")),
        check_vma=False,
    )
```
